32 devices in a mesh: dp: 8 (over y, x, core), ctx: 4 (over z).
Axes of the slice: x: 2, y: 2, z: 4, core: 2. Of those that a mesh axis runs over, the one named last changes fastest.
Arguments:
- tokens: bfloat16 [8192, 4096], P(('dp', 'ctx')), may hold values from -28 to 28
- projection: bfloat16 [4096, 3072], P('dp'), may hold values from -0.09375 to 0.09375
- placement: int32 [32, 32], P(('dp', 'ctx')), may hold values from 0 to 31, each once within a row
- doc_lengths: int32 [8, 8], P('dp'), may hold values from 1 to 512, 1024 in all within a row
Outputs:
- attended: bfloat16 [8192, 2048], P(('dp', 'ctx'))
The draws below stay inside these ranges and needn't reach their ends.
Inputs may be any that keep to these rules, and one draw needn't show every extreme that they name: `placement`: row i lists for each of the 8-row pieces of loader block i the device that computes it; every device appears once in each row. `doc_lengths`: each row holds the documents of one packed sequence of 1024 tokens in order, one of exactly 512 tokens.
All inputs are finite; a program needn't handle non-finite values.
Results may differ from the reference program's by a relative error of at most 0.006.
The reference program's roundings to bfloat16 on the way count: a program that leaves them out, or rounds other values in their place, can miss the bound.
Values may be sent and summed in bfloat16 or wider, within the bound.
A program may use at most 128 MiB of HBM per device.

```python
import math
from functools import partial
import jax
import jax.numpy as jnp
import numpy as np
from jax import lax

D = 4096
HEAD_DIM = 128
HEADS = 16
KV_HEADS = 4
DOCS = 8
SEQS = 8
SEQ = 1024
MOST = 512
PIECE = 8
TOKENS = 8192
QKV_W = 3072
DEVICES = 32


def draw_tokens(key, part):
    key = jax.random.fold_in(key, 11)
    former = jax.random.fold_in(key, 0)
    values = jnp.clip(jax.random.normal(former, (TOKENS, D), jnp.float32), -6.0, 6.0)
    return values.astype(jnp.bfloat16)


def shard_levels(rng, extent, cuts, low, largest):
    loudness = 1.0
    for axis_at, blocks in cuts:
        steps = jax.random.uniform(jax.random.fold_in(jax.random.fold_in(rng, 6), axis_at), (blocks,), jnp.float32, low / len(cuts), largest / len(cuts))
        loudness = loudness * jnp.repeat(jnp.exp(steps), extent[axis_at] // blocks).reshape((-1,) + (1,) * (len(extent) - 1 - axis_at))
    return loudness


def split_up(number_of, total, most, lean):
    weights = [(1 << 20) // math.isqrt(standing ** lean) + 1 for standing in range(2, number_of + 1)]
    spare, holding = total - most - (number_of - 1), [1] * (number_of - 1)
    while spare > 0:
        candidates = [i for i in range(number_of - 1) if holding[i] < most]
        pool, budget = sum([weights[i] for i in candidates]), spare
        for i in candidates:
            extra = min(most - holding[i], max(1, budget * weights[i] // pool), spare)
            holding[i] = holding[i] + extra
            spare = spare - extra
    return np.array([most] + holding)


def uneven_parts(rng, number_of, total, bound, slope):
    if number_of == 2:
        one = jax.random.randint(rng, (), max(1, total - bound), min(bound, total - 1) + 1)
        return jnp.stack([one, total - one])
    tallies = jnp.asarray(split_up(number_of, total, bound, slope), jnp.int32)
    twos = (number_of - 1) // 2
    source_of, receiver = tallies[1:1 + 2 * twos:2], tallies[2:2 + 2 * twos:2]
    margin = jnp.minimum(source_of - 1, bound - receiver)
    moved = jax.random.randint(jax.random.fold_in(rng, 1), (twos,), 0, 1 << 20) % (margin + 1)
    tallies = tallies.at[1:1 + 2 * twos:2].set(source_of - moved).at[2:2 + 2 * twos:2].set(receiver + moved)
    return tallies[jax.random.permutation(jax.random.fold_in(rng, 2), number_of)]


def bell_draw(rng, shape, scale, most, shards=(), held_as=jnp.bfloat16):
    level = shard_levels(rng, shape, shards, -0.22, 0.18) if shards else 1.0
    values = jax.random.normal(rng, shape, jnp.float32) * scale * level
    return jnp.minimum(jnp.maximum(values, -most), most).astype(held_as)


def setup_inputs(seed: int = 0) -> dict:
    keys = jax.random.split(jax.random.key(seed), 5)
    tokens = draw_tokens(jax.random.fold_in(keys[4], 71), 0)
    projection = bell_draw(keys[1], (D, QKV_W), D ** -0.5, 0.09375, ((0, 8),))
    placement = jax.vmap(lambda own: jax.random.permutation(own, DEVICES))(jax.random.split(keys[2], DEVICES)).reshape((DEVICES, DEVICES)).astype(jnp.int32)
    doc_lengths = jax.vmap(lambda own: uneven_parts(own, DOCS, SEQ, MOST, 2))(jax.random.split(keys[3], SEQS)).reshape((SEQS, DOCS)).astype(jnp.int32)
    return {"tokens": tokens, "projection": projection, "placement": placement, "doc_lengths": doc_lengths}


theta_base = 500000.0


def doc_tables(lengths, position):
    doc_ends = jnp.cumsum(lengths).astype(jnp.int32)
    doc_starts = doc_ends - lengths
    segment = jnp.sum((position[:, None] >= doc_ends[None, :]).astype(jnp.int32), axis=1)
    one_hot = segment[:, None] == jnp.arange(lengths.shape[0], dtype=jnp.int32)[None, :]
    begins = jnp.sum(jnp.where(one_hot, doc_starts[None, :], 0), axis=1).astype(jnp.int32)
    return segment, position - begins


def rotate(values, offsets, head_count):
    row_count = values.shape[0]
    half_dim = HEAD_DIM // 2
    frequency = theta_base ** (-2.0 * jnp.arange(half_dim, dtype=jnp.float32) / HEAD_DIM)
    angles = offsets.astype(jnp.float32)[:, None] * frequency[None, :]
    cosine = jnp.cos(angles)[:, None, :]
    sine = jnp.sin(angles)[:, None, :]
    halves = values.astype(jnp.float32).reshape(row_count, head_count, 2, half_dim)
    former = halves[:, :, 0]
    latter = halves[:, :, 1]
    result = jnp.stack([former * cosine - latter * sine, latter * cosine + former * sine], axis=2)
    return result.reshape(row_count, head_count * HEAD_DIM).astype(jnp.bfloat16)


def one_sequence(weight_matrix, inputs):
    rows_in, lengths = inputs
    projected = jnp.dot(rows_in, weight_matrix, preferred_element_type=jnp.float32).astype(jnp.bfloat16)
    position = jnp.arange(SEQ, dtype=jnp.int32)
    segment, offsets = doc_tables(lengths, position)
    query_width = HEADS * HEAD_DIM
    key_width = KV_HEADS * HEAD_DIM
    queries = rotate(projected[:, :query_width], offsets, HEADS)
    key_rows = rotate(projected[:, query_width:query_width + key_width], offsets, KV_HEADS)
    value_rows = projected[:, query_width + key_width:]
    group_size = HEADS // KV_HEADS
    query_heads = queries.astype(jnp.float32).reshape(SEQ, KV_HEADS, group_size, HEAD_DIM)
    key_heads = key_rows.astype(jnp.float32).reshape(SEQ, KV_HEADS, HEAD_DIM)
    value_heads = value_rows.astype(jnp.float32).reshape(SEQ, KV_HEADS, HEAD_DIM)
    scores = jnp.einsum("tkgd,skd->tkgs", query_heads, key_heads) * (HEAD_DIM ** -0.5)
    allowed = (segment[:, None] == segment[None, :]) & (position[None, :] <= position[:, None])
    scores = jnp.where(allowed[:, None, None, :], scores, -jnp.inf)
    row_max = jnp.max(scores, axis=-1, keepdims=True)
    weights = jnp.exp(scores - row_max)
    row_sum = jnp.sum(weights, axis=-1)
    rounded = lax.optimization_barrier(weights.astype(jnp.bfloat16)).astype(jnp.float32)
    mixed = jnp.einsum("tkgs,skd->tkgd", rounded, value_heads) / row_sum[..., None]
    return mixed.reshape(SEQ, HEADS * HEAD_DIM).astype(jnp.bfloat16)


def reference(tokens, projection, placement, doc_lengths):
    home_rows = tokens.reshape(DEVICES, DEVICES, PIECE, D)
    source = jnp.broadcast_to(jnp.arange(DEVICES, dtype=jnp.int32)[:, None], (DEVICES, DEVICES))
    work_rows = jnp.zeros_like(home_rows).at[placement, source].set(home_rows)
    grouped = work_rows.reshape(SEQS, SEQ, D)
    mixed = lax.map(partial(one_sequence, projection), (grouped, doc_lengths))
    mixed = mixed.reshape(DEVICES, DEVICES, PIECE, HEADS * HEAD_DIM)
    return mixed[placement, source].reshape(TOKENS, HEADS * HEAD_DIM)
```

```python
import functools
import math

import jax
import jax.numpy as jnp
from jax import lax
from jax.experimental import pallas as pl
from jax.experimental.pallas import tpu as pltpu
from jax.sharding import PartitionSpec as P

HEAD_DIM = 128
HEADS = 16
KV_HEADS = 4
GROUP = HEADS // KV_HEADS
Q_W = GROUP * HEAD_DIM
PART_W = Q_W + 2 * HEAD_DIM
MOST = 512
MESH = pl.DeviceIdType.MESH

theta_base = 500000.0


def position_tables(lengths, seq):
    position = jnp.arange(seq, dtype=jnp.int32)
    ends = jnp.cumsum(lengths)
    begins = jnp.max(
        jnp.where(position[:, None] >= ends[None, :], ends[None, :], 0), axis=1
    )
    half = HEAD_DIM // 2
    frequency = theta_base ** (-2.0 * jnp.arange(half, dtype=jnp.float32) / HEAD_DIM)
    angles = (position - begins).astype(jnp.float32)[:, None] * frequency[None, :]
    cosine, sine = jnp.cos(angles), jnp.sin(angles)
    return (
        jnp.concatenate([cosine, cosine], axis=1),
        jnp.concatenate([-sine, sine], axis=1),
        jnp.broadcast_to(begins[:, None], (seq, HEAD_DIM)),
    )


def attention_kernel(block, proj_ref, cos_ref, sin_ref, begin_ref, out_ref, key_ref):
    seq = proj_ref.shape[0]
    factor = HEAD_DIM**-0.5 * math.log2(math.e)

    def rotated(rows, column):
        x = proj_ref[rows, column : column + HEAD_DIM].astype(jnp.float32)
        turned = pltpu.roll(x, HEAD_DIM // 2, 1)
        return (x * cos_ref[rows, :] + turned * sin_ref[rows, :]).astype(jnp.bfloat16)

    for b in range(seq // block):
        rows = slice(b * block, (b + 1) * block)
        key_ref[rows, :] = rotated(rows, Q_W)
    for b in range(seq // block):
        rows = slice(b * block, (b + 1) * block)
        first = max(0, (b * block - (MOST - 1)) // block * block)
        keys = slice(first, (b + 1) * block)
        width = (b + 1) * block - first
        at = first + lax.broadcasted_iota(jnp.int32, (block, width), 1)
        own = b * block + lax.broadcasted_iota(jnp.int32, (block, width), 0)
        allowed = (at >= begin_ref[rows, 0:1]) & (at <= own)
        values = proj_ref[keys, Q_W + HEAD_DIM : PART_W]
        for h in range(GROUP):
            scores = lax.dot_general(
                rotated(rows, h * HEAD_DIM),
                key_ref[keys, :],
                (((1,), (1,)), ((), ())),
                preferred_element_type=jnp.float32,
            )
            scores = jnp.where(allowed, scores, -jnp.inf)
            top = jnp.max(scores, axis=1, keepdims=True)
            weights = jnp.exp2((scores - top) * factor)
            total = jnp.sum(weights, axis=1, keepdims=True)
            mixed = jnp.dot(
                weights.astype(jnp.bfloat16), values, preferred_element_type=jnp.float32
            )
            out_ref[rows, h * HEAD_DIM : (h + 1) * HEAD_DIM] = (mixed / total).astype(jnp.bfloat16)


def attention(projected, lengths):
    seq = projected.shape[0]
    cosine, sine, begins = position_tables(lengths, seq)
    return pl.pallas_call(
        functools.partial(attention_kernel, 256),
        out_shape=jax.ShapeDtypeStruct((seq, Q_W), jnp.bfloat16),
        in_specs=[pl.BlockSpec(memory_space=pltpu.VMEM)] * 4,
        out_specs=pl.BlockSpec(memory_space=pltpu.VMEM),
        scratch_shapes=[pltpu.VMEM((seq, HEAD_DIM), jnp.bfloat16)],
        compiler_params=pltpu.CompilerParams(vmem_limit_bytes=32 * 2**20),
    )(projected, cosine, sine, begins)


def gather_kernel(dp, ctx, chunk, tok_ref, w_ref, out_ref, x_ref, w_buf, acc_ref,
                  own_sem, wown_sem, tok_send, tok_recv, z_send, z_recv, c_send, c_recv, w_send, w_recv):
    d, c = lax.axis_index("dp"), lax.axis_index("ctx")
    dc, cz = d % 2, c % 2
    groups = dp * ctx // 4
    halves = ctx // 2
    s_me = (d // 2) * halves + c // 2
    m_me = dc * 2 + cz
    m_z = dc * 2 + 1 - cz
    d_sib, c_sib = d + 1 - 2 * dc, c + 1 - 2 * cz
    slab = groups * chunk
    depth = w_ref.shape[0]

    def class_peer(s):
        return ((s // halves) * 2 + dc, (s % halves) * 2 + cz)

    barrier = pltpu.get_barrier_semaphore()
    met = 0
    for t in range(1, groups):
        pl.semaphore_signal(barrier, inc=1, device_id=class_peer((s_me + t) % groups), device_id_type=MESH)
        met += 1
    for t in range(dp // 2):
        other = ((d // 2 + t) % (dp // 2)) * 2 + 1 - dc
        pl.semaphore_signal(barrier, inc=1, device_id=(other, c), device_id_type=MESH)
        met += 1
    pl.semaphore_signal(barrier, inc=1, device_id=(d, c_sib), device_id_type=MESH)
    pl.semaphore_wait(barrier, met + 1)

    def x_rows(m, s):
        return x_ref.at[pl.ds(pl.multiple_of(m * slab + s * chunk, chunk), chunk), :]

    def tok_rows(s):
        return tok_ref.at[pl.ds(pl.multiple_of(s * chunk, chunk), chunk), :]

    def remote(src, dst, send, recv, device):
        return pltpu.make_async_remote_copy(
            src_ref=src, dst_ref=dst, send_sem=send, recv_sem=recv, device_id=device, device_id_type=MESH
        )

    own = pltpu.make_async_copy(tok_rows(s_me), x_rows(m_me, s_me), own_sem)
    own.start()

    def tok_copy(t):
        s = (s_me + t) % groups
        return remote(tok_rows(s), x_rows(m_me, s_me), tok_send.at[t], tok_recv.at[t], class_peer(s))

    for t in range(1, groups):
        tok_copy(t).start()

    parts = ((0, 0, Q_W), (HEADS * HEAD_DIM, Q_W, HEAD_DIM),
             ((HEADS + KV_HEADS) * HEAD_DIM, Q_W + HEAD_DIM, HEAD_DIM))

    def w_pieces(d_to, d_from):
        g = (d_to % 2) * 2 + cz
        for base, to, width in parts:
            yield (w_ref.at[:, pl.ds(pl.multiple_of(base + g * width, HEAD_DIM), width)],
                   w_buf.at[d_from, :, to : to + width])

    def w_copies(t):
        d_to = (d + t) % dp
        return [remote(src, dst, w_send.at[t, i], w_recv.at[t, i], (d_to, c))
                for i, (src, dst) in enumerate(w_pieces(d_to, d))]

    w_own = [pltpu.make_async_copy(src, dst, wown_sem.at[i]) for i, (src, dst) in enumerate(w_pieces(d, d))]
    for copy in w_own:
        copy.start()
    for t in range(1, dp):
        for copy in w_copies(t):
            copy.start()

    def z_copy(t):
        s = (s_me - t + groups) % groups
        return remote(x_rows(m_me, s), x_rows(m_me, s), z_send.at[t], z_recv.at[t], (d, c_sib))

    def z_arrival(t):
        s = (s_me - t + groups) % groups
        return remote(x_rows(m_z, s), x_rows(m_z, s), z_send.at[t], z_recv.at[t], (d, c_sib))

    def c_copy(which, t):
        s = (s_me - t + groups) % groups
        m = m_me if which == 0 else m_z
        return remote(x_rows(m, s), x_rows(m, s), c_send.at[which, t], c_recv.at[which, t], (d_sib, c))

    def c_arrival(which, t):
        s = (s_me - t + groups) % groups
        m = (1 - dc) * 2 + (cz if which == 0 else 1 - cz)
        return remote(x_rows(m, s), x_rows(m, s), c_send.at[which, t], c_recv.at[which, t], (d_sib, c))

    own.wait()
    for t in range(groups):
        if t > 0:
            s = (s_me - t + groups) % groups
            remote(tok_rows(s), x_rows(m_me, s), tok_send.at[t], tok_recv.at[t], class_peer(s)).wait_recv()
        z_copy(t).start()
        c_copy(0, t).start()
    for t in range(groups):
        z_arrival(t).wait_recv()
        c_copy(1, t).start()

    def multiply(m, d_from):
        rows = pl.ds(pl.multiple_of(m * slab, slab), slab)
        columns = pl.ds(pl.multiple_of(d_from * depth, depth), depth)
        return jnp.dot(x_ref[rows, columns], w_buf[d_from], preferred_element_type=jnp.float32)

    def acc_rows(m):
        return pl.ds(pl.multiple_of(m * slab, slab), slab)

    for copy in w_own:
        copy.wait()
    for t in range(dp):
        d_from = (d - t + dp) % dp
        if t > 0:
            for i, (src, dst) in enumerate(w_pieces(d, d_from)):
                remote(src, dst, w_send.at[t, i], w_recv.at[t, i], (d_from, c)).wait_recv()
        for m in (m_me, m_z):
            if t == 0:
                acc_ref[acc_rows(m), :] = multiply(m, d_from)
            else:
                acc_ref[acc_rows(m), :] += multiply(m, d_from)
    for which in range(2):
        for t in range(groups):
            c_arrival(which, t).wait_recv()
        m = (1 - dc) * 2 + (cz if which == 0 else 1 - cz)
        acc_ref[acc_rows(m), :] = multiply(m, 0)

        @pl.loop(1, dp)
        def _(k):
            acc_ref[acc_rows(m), :] += multiply(m, k)

    piece = chunk // ctx
    block = dp * ctx * piece

    def rows_of(i, q):
        src_d, src_c = i // ctx, i % ctx
        m = (src_d % 2) * 2 + src_c % 2
        s = (src_d // 2) * halves + src_c // 2
        start = pl.multiple_of(m * slab + s * chunk + q * piece, piece)
        return acc_ref[pl.ds(start, piece), :]

    @pl.loop(0, dp * ctx // 2)
    def _(pair):
        for q in range(ctx):
            both = jnp.concatenate([rows_of(pair * 2, q), rows_of(pair * 2 + 1, q)], axis=0)
            to = pl.multiple_of(q * block + pair * 2 * piece, 2 * piece)
            out_ref[pl.ds(to, 2 * piece), :] = both.astype(jnp.bfloat16)

    for t in range(groups):
        if t > 0:
            tok_copy(t).wait_send()
        z_copy(t).wait_send()
        c_copy(0, t).wait_send()
        c_copy(1, t).wait_send()
    for t in range(1, dp):
        for copy in w_copies(t):
            copy.wait_send()


def gathered_projection(outgoing, weights, dp, ctx):
    rows, width = outgoing.shape
    depth = weights.shape[0]
    groups = dp * ctx // 4
    chunk = rows // groups
    seq = 4 * groups * chunk
    dma = pltpu.SemaphoreType.DMA
    return pl.pallas_call(
        functools.partial(gather_kernel, dp, ctx, chunk),
        out_shape=jax.ShapeDtypeStruct((seq, PART_W), jnp.bfloat16),
        in_specs=[pl.BlockSpec(memory_space=pl.ANY)] * 2,
        out_specs=pl.BlockSpec(memory_space=pltpu.VMEM),
        scratch_shapes=[
            pltpu.VMEM((seq, width), jnp.bfloat16),
            pltpu.VMEM((dp, depth, PART_W), jnp.bfloat16),
            pltpu.VMEM((seq, PART_W), jnp.float32),
            dma, dma((3,)),
            dma((groups,)), dma((groups,)),
            dma((groups,)), dma((groups,)),
            dma((2, groups)), dma((2, groups)),
            dma((dp, 3)), dma((dp, 3)),
        ],
        compiler_params=pltpu.CompilerParams(
            collective_id=0, has_side_effects=True, vmem_limit_bytes=48 * 2**20
        ),
    )(outgoing, weights)


def on_device(dp, ctx, tokens, projection, placement, doc_lengths):
    row_count, width = tokens.shape
    dev_count = placement.shape[1]
    piece_rows = row_count // dev_count
    destinations = placement[0]
    slot_of = (
        jnp.zeros((dev_count,), jnp.int32)
        .at[destinations]
        .set(jnp.arange(dev_count, dtype=jnp.int32))
    )
    outgoing = tokens.reshape(dev_count, piece_rows, width)[slot_of]
    depth = projection.shape[0]
    direct = piece_rows == 8 and ctx == 4 and depth % 256 == 0
    d, c = lax.axis_index("dp"), lax.axis_index("ctx")
    seq_index = (d // 2) * 2 + c // 2
    if direct:
        projected = gathered_projection(outgoing.reshape(row_count, width), projection, dp, ctx)
        all_lengths = lax.all_gather(doc_lengths, "dp", axis=0, tiled=True)
        lengths = lax.dynamic_index_in_dim(all_lengths, seq_index, 0, keepdims=False)
    else:
        arrived = lax.all_to_all(outgoing, ("dp", "ctx"), split_axis=0, concat_axis=0, tiled=True)
        rows = lax.all_gather(arrived.reshape(row_count, width), "ctx", axis=0, tiled=True)
        cuts = [
            lax.dynamic_slice_in_dim(projection, base + c * w, w, axis=1)
            for base, w in ((0, Q_W), (HEADS * HEAD_DIM, HEAD_DIM), ((HEADS + KV_HEADS) * HEAD_DIM, HEAD_DIM))
        ]
        weights = lax.all_gather(jnp.concatenate(cuts, axis=1), "dp", axis=0, tiled=True)
        projected = jnp.dot(rows, weights, preferred_element_type=jnp.float32).astype(jnp.bfloat16)
        lengths = doc_lengths[0]
    mixed = attention(projected, lengths)
    by_source = jnp.transpose(mixed.reshape(ctx, dev_count, piece_rows, Q_W), (1, 0, 2, 3))
    returned = lax.all_to_all(by_source, ("dp", "ctx"), split_axis=0, concat_axis=0, tiled=True)
    if direct:
        parts = returned.reshape(dp // 2, 2, ctx // 2, 2, ctx, piece_rows, Q_W)
        parts = jnp.transpose(parts, (0, 2, 4, 5, 1, 3, 6))
    else:
        parts = returned.reshape(dp, ctx, ctx, piece_rows, Q_W)
        parts = jnp.transpose(parts, (0, 2, 3, 1, 4))
    blocks = parts.reshape(dev_count, piece_rows, HEADS * HEAD_DIM)
    return blocks[destinations].reshape(row_count, HEADS * HEAD_DIM)


def solution(mesh):
    return jax.shard_map(
        functools.partial(on_device, mesh.shape["dp"], mesh.shape["ctx"]),
        mesh=mesh,
        in_specs=(P(("dp", "ctx"), None), P("dp", None), P(("dp", "ctx"), None), P("dp", None)),
        out_specs=P(("dp", "ctx"), None),
        check_vma=False,
    )
```

```python
import functools
import math

import jax
import jax.numpy as jnp
from jax import lax
from jax.experimental import pallas as pl
from jax.experimental.pallas import tpu as pltpu
from jax.sharding import PartitionSpec as P

HEAD_DIM = 128
HEADS = 16
KV_HEADS = 4
GROUP = HEADS // KV_HEADS
Q_W = GROUP * HEAD_DIM
PART_W = Q_W + 2 * HEAD_DIM
MOST = 512
MESH = pl.DeviceIdType.MESH

theta_base = 500000.0


def position_tables(lengths, seq):
    position = jnp.arange(seq, dtype=jnp.int32)
    ends = jnp.cumsum(lengths)
    begins = jnp.max(
        jnp.where(position[:, None] >= ends[None, :], ends[None, :], 0), axis=1
    )
    half = HEAD_DIM // 2
    frequency = theta_base ** (-2.0 * jnp.arange(half, dtype=jnp.float32) / HEAD_DIM)
    angles = (position - begins).astype(jnp.float32)[:, None] * frequency[None, :]
    cosine, sine = jnp.cos(angles), jnp.sin(angles)
    return (
        jnp.concatenate([cosine, cosine], axis=1),
        jnp.concatenate([-sine, sine], axis=1),
        jnp.broadcast_to(begins[:, None].astype(jnp.float32), (seq, HEAD_DIM)),
    )


def attention_kernel(block, proj_ref, cos_ref, sin_ref, begin_ref, out_ref, key_ref):
    seq = proj_ref.shape[0]
    factor = HEAD_DIM**-0.5 * math.log2(math.e)

    def rotated(rows, column):
        x = proj_ref[rows, column : column + HEAD_DIM].astype(jnp.float32)
        turned = pltpu.roll(x, HEAD_DIM // 2, 1)
        return (x * cos_ref[rows, :] + turned * sin_ref[rows, :]).astype(jnp.bfloat16)

    for b in range(seq // block):
        rows = slice(b * block, (b + 1) * block)
        key_ref[rows, :] = rotated(rows, Q_W)
    for b in range(seq // block):
        rows = slice(b * block, (b + 1) * block)
        first = max(0, (b * block - (MOST - 1)) // block * block)
        keys = slice(first, (b + 1) * block)
        width = (b + 1) * block - first
        at = first + lax.broadcasted_iota(jnp.int32, (block, width), 1)
        own = b * block + lax.broadcasted_iota(jnp.int32, (block, width), 0)
        allowed = (at.astype(jnp.float32) >= begin_ref[rows, 0:1]) & (at <= own)
        values = proj_ref[keys, Q_W + HEAD_DIM : PART_W]
        for h in range(GROUP):
            scores = lax.dot_general(
                rotated(rows, h * HEAD_DIM),
                key_ref[keys, :],
                (((1,), (1,)), ((), ())),
                preferred_element_type=jnp.float32,
            )
            scores = jnp.where(allowed, scores, -jnp.inf)
            top = jnp.max(scores, axis=1, keepdims=True)
            weights = jnp.exp2((scores - top) * factor)
            total = jnp.sum(weights, axis=1, keepdims=True)
            mixed = jnp.dot(
                weights.astype(jnp.bfloat16), values, preferred_element_type=jnp.float32
            )
            out_ref[rows, h * HEAD_DIM : (h + 1) * HEAD_DIM] = (mixed / total).astype(jnp.bfloat16)


def attention(projected, lengths):
    seq = projected.shape[0]
    cosine, sine, begins = position_tables(lengths, seq)
    return pl.pallas_call(
        functools.partial(attention_kernel, 256),
        out_shape=jax.ShapeDtypeStruct((seq, Q_W), jnp.bfloat16),
        in_specs=[pl.BlockSpec(memory_space=pltpu.VMEM)] * 4,
        out_specs=pl.BlockSpec(memory_space=pltpu.VMEM),
        scratch_shapes=[pltpu.VMEM((seq, HEAD_DIM), jnp.bfloat16)],
        compiler_params=pltpu.CompilerParams(vmem_limit_bytes=32 * 2**20),
    )(projected, cosine, sine, begins)


PHASES = (
    ((HEADS * HEAD_DIM, HEAD_DIM, 0, HEAD_DIM), ((HEADS + KV_HEADS) * HEAD_DIM, HEAD_DIM, HEAD_DIM, HEAD_DIM),
     (0, Q_W, 2 * HEAD_DIM, Q_W // 2)),
    ((Q_W // 2, Q_W, 2 * HEAD_DIM + Q_W // 2, Q_W // 2),),
)
PHASE_COLUMNS = ((0, 2 * HEAD_DIM + Q_W // 2), (2 * HEAD_DIM + Q_W // 2, Q_W // 2))
RET_W = Q_W // 2


def whole_kernel(dp, ctx, chunk, tok_ref, w_ref, tab_ref, ret_ref,
                 x_ref, w_buf, acc_ref, key_ref, val_ref, qry_ref, mix_ref, out_buf, tabs,
                 own_sem, wown_sem, tab_own, tab_send, tab_recv, tok_send, tok_recv, z_send, z_recv,
                 c_send, c_recv, w_send, w_recv, f_send, f_recv, r_own, r_send, r_recv):
    d, c = lax.axis_index("dp"), lax.axis_index("ctx")
    devices = dp * ctx
    me = d * ctx + c
    dc, cz = d % 2, c % 2
    groups = devices // 4
    halves = ctx // 2
    s_me = (d // 2) * halves + c // 2
    m_me = dc * 2 + cz
    m_z = dc * 2 + 1 - cz
    d_sib, c_sib = d + 1 - 2 * dc, c + 1 - 2 * cz
    slab = groups * chunk
    depth = w_ref.shape[0]
    piece = chunk // ctx
    block = devices * piece
    seq = ctx * block

    def class_peer(s):
        return ((s // halves) * 2 + dc, (s % halves) * 2 + cz)

    def remote(src, dst, send, recv, device):
        return pltpu.make_async_remote_copy(
            src_ref=src, dst_ref=dst, send_sem=send, recv_sem=recv, device_id=device, device_id_type=MESH
        )

    barrier = pltpu.get_barrier_semaphore()

    @pl.loop(1, devices)
    def _(t):
        other = (me + t) % devices
        pl.semaphore_signal(barrier, inc=1, device_id=(other // ctx, other % ctx), device_id_type=MESH)

    pl.semaphore_wait(barrier, devices - 1)

    def x_rows(m, s):
        return x_ref.at[pl.ds(pl.multiple_of(m * slab + s * chunk, chunk), chunk), :]

    def tok_rows(s):
        return tok_ref.at[pl.ds(pl.multiple_of(s * chunk, chunk), chunk), :]

    own = pltpu.make_async_copy(tok_rows(s_me), x_rows(m_me, s_me), own_sem)
    own.start()

    def tok_copy(t):
        s = (s_me + t) % groups
        return remote(tok_rows(s), x_rows(m_me, s_me), tok_send.at[t], tok_recv.at[t], class_peer(s))

    for t in range(1, groups):
        tok_copy(t).start()

    tab_mine = pltpu.make_async_copy(tab_ref, tabs.at[dc], tab_own)
    tab_mine.start()
    tab_out = remote(tab_ref, tabs.at[dc], tab_send, tab_recv, (d_sib, c))
    tab_out.start()
    tab_in = remote(tab_ref, tabs.at[1 - dc], tab_send, tab_recv, (d_sib, c))

    chip = d // 2
    chip_x = chip + 1 - 2 * (chip % 2)
    chip_y = (chip + 2) % 4
    chip_far = (chip_x + 2) % 4

    def w_parts(d_to, d_from, phase):
        g = (d_to % 2) * 2 + cz
        for i, (base, stride, to, width) in enumerate(PHASES[phase]):
            start = pl.multiple_of(base + g * stride, HEAD_DIM)
            yield (w_ref.at[:, pl.ds(start, width)], w_buf.at[d_from, :, to : to + width], 3 * phase + i)

    near = ((0, d_sib), (1, chip_x * 2 + dc), (2, chip_x * 2 + 1 - dc), (3, chip_y * 2 + dc), (4, chip_y * 2 + 1 - dc))

    def w_out(phase):
        return [remote(src, dst, w_send.at[slot, i], w_recv.at[slot, i], (d_to, c))
                for slot, d_to in near for src, dst, i in w_parts(d_to, d, phase)]

    def w_in(phase, slots):
        return [remote(src, dst, w_send.at[slot, i], w_recv.at[slot, i], (d_from, c))
                for slot, d_from in near if slot in slots for src, dst, i in w_parts(d, d_from, phase)]

    w_own = [pltpu.make_async_copy(src, dst, wown_sem.at[i])
             for phase in range(2) for src, dst, i in w_parts(d, d, phase)]

    half = depth // 2

    def f_parts(chip_from, way, phase, chip_to):
        for core in range(2):
            for i, (_, _, to, width) in enumerate(PHASES[phase]):
                there = w_buf.at[chip_from * 2 + core, way * half : (way + 1) * half, to : to + width]
                yield remote(there, there, f_send.at[way, core, 3 * phase + i], f_recv.at[way, core, 3 * phase + i],
                             (chip_to * 2 + dc, c))

    def f_out(phase, way):
        return list(f_parts((chip_x, chip_y)[way], way, phase, (chip_y, chip_x)[way]))

    def f_in(phase, way):
        return list(f_parts(chip_far, way, phase, (chip_y, chip_x)[way]))

    for copy in w_out(0):
        copy.start()
    for copy in w_own:
        copy.start()
    for copy in w_out(1):
        copy.start()

    def came(t):
        return (s_me - t + groups) % groups

    def z_copy(t):
        return remote(x_rows(m_me, came(t)), x_rows(m_me, came(t)), z_send.at[t], z_recv.at[t], (d, c_sib))

    def z_arrival(t):
        return remote(x_rows(m_z, came(t)), x_rows(m_z, came(t)), z_send.at[t], z_recv.at[t], (d, c_sib))

    def c_copy(which, t):
        at = x_rows(m_z if which else m_me, came(t))
        return remote(at, at, c_send.at[which, t], c_recv.at[which, t], (d_sib, c))

    def c_arrival(which, t):
        at = x_rows((1 - dc) * 2 + (1 - cz if which else cz), came(t))
        return remote(at, at, c_send.at[which, t], c_recv.at[which, t], (d_sib, c))

    own.wait()
    for t in range(groups):
        if t > 0:
            remote(tok_rows(came(t)), x_rows(m_me, came(t)), tok_send.at[t], tok_recv.at[t],
                   class_peer(came(t))).wait_recv()
        z_copy(t).start()
        c_copy(0, t).start()

    def forward_weights(phase):
        for way in range(2):
            for copy in w_in(phase, ((1, 2), (3, 4))[way]):
                copy.wait_recv()
            for copy in f_out(phase, way):
                copy.start()

    for t in range(groups):
        if t == groups // 2:
            forward_weights(0)
        z_arrival(t).wait_recv()
        c_copy(1, t).start()
    forward_weights(1)

    def multiply(m, phase):
        rows = pl.ds(pl.multiple_of(m * slab, slab), slab)
        first, width = PHASE_COLUMNS[phase]

        def product(k):
            columns = pl.ds(pl.multiple_of(k * depth, depth), depth)
            return jnp.dot(x_ref[rows, columns], w_buf[k, :, first : first + width],
                           preferred_element_type=jnp.float32)

        acc_ref[rows, 0:width] = product(0)

        @pl.loop(1, dp)
        def _(k):
            acc_ref[rows, 0:width] += product(k)

    def rows_of(i, q, first, width):
        src_d, src_c = i // ctx, i % ctx
        m = (src_d % 2) * 2 + src_c % 2
        s = (src_d // 2) * halves + src_c // 2
        start = pl.multiple_of(m * slab + s * chunk + q * piece, piece)
        return acc_ref[pl.ds(start, piece), first : first + width]

    seq_slot = c // 2

    def rotate(x, at):
        x = x.astype(jnp.bfloat16).astype(jnp.float32)
        turned = pltpu.roll(x, HEAD_DIM // 2, 1)
        cosine = tabs[seq_slot, pl.ds(at, 2 * piece), :]
        sine = tabs[seq_slot, pl.ds(pl.multiple_of(seq + at, 2 * piece), 2 * piece), :]
        return (x * cosine + turned * sine).astype(jnp.bfloat16)

    def pack(phase):
        @pl.loop(0, devices // 2)
        def _(pair):
            for q in range(ctx):
                def both(first):
                    return jnp.concatenate(
                        [rows_of(pair * 2 + i, q, first, HEAD_DIM) for i in range(2)], axis=0)

                at = pl.multiple_of(q * block + pair * 2 * piece, 2 * piece)
                to = pl.ds(at, 2 * piece)
                if phase == 0:
                    key_ref[to, :] = rotate(both(0), at)
                    val_ref[to, :] = both(HEAD_DIM).astype(jnp.bfloat16)
                base = 2 * HEAD_DIM if phase == 0 else 0
                for h in range(GROUP // 2):
                    qry_ref[to, h * HEAD_DIM : (h + 1) * HEAD_DIM] = rotate(both(base + h * HEAD_DIM), at)

    factor = HEAD_DIM**-0.5 * math.log2(math.e)

    def attend():
        for b in range(ctx):
            rows = slice(b * block, (b + 1) * block)
            first = max(0, (b * block - (MOST - 1)) // block * block)
            keys = slice(first, (b + 1) * block)
            width = (b + 1) * block - first
            at = first + lax.broadcasted_iota(jnp.int32, (block, width), 1)
            at_own = b * block + lax.broadcasted_iota(jnp.int32, (block, width), 0)
            begin = tabs[seq_slot, 2 * seq + b * block : 2 * seq + (b + 1) * block, 0:1]
            allowed = (at.astype(jnp.float32) >= begin) & (at <= at_own)
            for h in range(GROUP // 2):
                scores = lax.dot_general(
                    qry_ref[rows, h * HEAD_DIM : (h + 1) * HEAD_DIM], key_ref[keys, :],
                    (((1,), (1,)), ((), ())), preferred_element_type=jnp.float32,
                )
                scores = jnp.where(allowed, scores, -jnp.inf)
                top = jnp.max(scores, axis=1, keepdims=True)
                weights = jnp.exp2((scores - top) * factor)
                total = jnp.sum(weights, axis=1, keepdims=True)
                mixed = jnp.dot(weights.astype(jnp.bfloat16), val_ref[keys, :],
                                preferred_element_type=jnp.float32)
                mix_ref[rows, h * HEAD_DIM : (h + 1) * HEAD_DIM] = mixed / total

    def ret_at(s, m, phase):
        return ret_ref.at[pl.ds(pl.multiple_of(s * chunk, chunk), chunk),
                          pl.ds(pl.multiple_of(m * Q_W + phase * RET_W, RET_W), RET_W)]

    def buf_at(i, phase):
        return out_buf.at[phase, pl.ds(pl.multiple_of(i * chunk, chunk), chunk), :]

    def ret_copy(phase, t):
        i = (me + t) % devices
        return remote(buf_at(i, phase), ret_at(s_me, m_me, phase), r_send.at[phase, t], r_recv.at[phase, t],
                      (i // ctx, i % ctx))

    def ret_arrival(phase, t):
        i = (me - t + devices) % devices
        src_d, src_c = i // ctx, i % ctx
        s = (src_d // 2) * halves + src_c // 2
        m = (src_d % 2) * 2 + src_c % 2
        return remote(buf_at(i, phase), ret_at(s, m, phase), r_send.at[phase, t], r_recv.at[phase, t],
                      (src_d, src_c))

    def own_ret(phase):
        return pltpu.make_async_copy(buf_at(me, phase), ret_at(s_me, m_me, phase), r_own.at[phase])

    def send_back(phase):
        def ready(i):
            parts = [mix_ref[pl.ds(pl.multiple_of(q * block + i * piece, piece), piece), :] for q in range(ctx)]
            out_buf[phase, pl.ds(pl.multiple_of(i * chunk, chunk), chunk), :] = (
                jnp.concatenate(parts, axis=0).astype(jnp.bfloat16))

        @pl.loop(1, devices)
        def _(t):
            ready((me + t) % devices)
            ret_copy(phase, t).start()

        ready(me)
        own_ret(phase).start()

    tab_mine.wait()
    tab_in.wait_recv()
    for copy in w_own:
        copy.wait()
    for phase in range(2):
        for copy in w_in(phase, (0,)) + f_in(phase, 0) + f_in(phase, 1):
            copy.wait_recv()
        multiply(m_me, phase)
        multiply(m_z, phase)
        for which in range(2):
            if phase == 0:
                for t in range(groups):
                    c_arrival(which, t).wait_recv()
            multiply((1 - dc) * 2 + (1 - cz if which else cz), phase)
        pack(phase)
        attend()
        send_back(phase)

    tab_out.wait_send()
    for t in range(groups):
        if t > 0:
            tok_copy(t).wait_send()
        z_copy(t).wait_send()
        c_copy(0, t).wait_send()
        c_copy(1, t).wait_send()
    for phase in range(2):
        for copy in w_out(phase) + f_out(phase, 0) + f_out(phase, 1):
            copy.wait_send()
        own_ret(phase).wait()

        @pl.loop(1, devices)
        def _(t):
            ret_copy(phase, t).wait_send()
            ret_arrival(phase, t).wait_recv()


def attended_blocks(outgoing, weights, tables, dp, ctx):
    rows, width = outgoing.shape
    depth = weights.shape[0]
    devices = dp * ctx
    groups = devices // 4
    chunk = rows // groups
    seq = 4 * rows
    dma = pltpu.SemaphoreType.DMA
    return pl.pallas_call(
        functools.partial(whole_kernel, dp, ctx, chunk),
        out_shape=jax.ShapeDtypeStruct((rows, HEADS * HEAD_DIM), jnp.bfloat16),
        in_specs=[pl.BlockSpec(memory_space=pl.ANY)] * 3,
        out_specs=pl.BlockSpec(memory_space=pl.ANY),
        scratch_shapes=[
            pltpu.VMEM((seq, width), jnp.bfloat16),
            pltpu.VMEM((dp, depth, PART_W), jnp.bfloat16),
            pltpu.VMEM((seq, PHASE_COLUMNS[0][1]), jnp.float32),
            pltpu.VMEM((seq, HEAD_DIM), jnp.bfloat16),
            pltpu.VMEM((seq, HEAD_DIM), jnp.bfloat16),
            pltpu.VMEM((seq, RET_W), jnp.bfloat16),
            pltpu.VMEM((seq, RET_W), jnp.float32),
            pltpu.VMEM((2, seq, RET_W), jnp.bfloat16),
            pltpu.VMEM((2, 3 * seq, HEAD_DIM), jnp.float32),
            dma, dma((4,)), dma, dma, dma,
            dma((groups,)), dma((groups,)),
            dma((groups,)), dma((groups,)),
            dma((2, groups)), dma((2, groups)),
            dma((5, 4)), dma((5, 4)),
            dma((2, 2, 4)), dma((2, 2, 4)),
            dma((2,)), dma((2, devices)), dma((2, devices)),
        ],
        compiler_params=pltpu.CompilerParams(
            collective_id=0, has_side_effects=True, vmem_limit_bytes=48 * 2**20
        ),
    )(outgoing, weights, tables)


def on_device(dp, ctx, tokens, projection, placement, doc_lengths):
    row_count, width = tokens.shape
    dev_count = placement.shape[1]
    piece_rows = row_count // dev_count
    destinations = placement[0]
    slot_of = (
        jnp.zeros((dev_count,), jnp.int32)
        .at[destinations]
        .set(jnp.arange(dev_count, dtype=jnp.int32))
    )
    outgoing = tokens.reshape(dev_count, piece_rows, width)[slot_of]
    depth = projection.shape[0]
    if dp == 8 and ctx == 4 and piece_rows == 8:
        tables = jnp.concatenate(position_tables(doc_lengths[0], ctx * row_count), axis=0)
        blocks = attended_blocks(outgoing.reshape(row_count, width), projection, tables, dp, ctx)
    else:
        c = lax.axis_index("ctx")
        arrived = lax.all_to_all(outgoing, ("dp", "ctx"), split_axis=0, concat_axis=0, tiled=True)
        rows = lax.all_gather(arrived.reshape(row_count, width), "ctx", axis=0, tiled=True)
        cuts = [
            lax.dynamic_slice_in_dim(projection, base + c * w, w, axis=1)
            for base, w in ((0, Q_W), (HEADS * HEAD_DIM, HEAD_DIM), ((HEADS + KV_HEADS) * HEAD_DIM, HEAD_DIM))
        ]
        weights = lax.all_gather(jnp.concatenate(cuts, axis=1), "dp", axis=0, tiled=True)
        projected = jnp.dot(rows, weights, preferred_element_type=jnp.float32).astype(jnp.bfloat16)
        mixed = attention(projected, doc_lengths[0])
        by_source = jnp.transpose(mixed.reshape(ctx, dev_count, piece_rows, Q_W), (1, 0, 2, 3))
        returned = lax.all_to_all(by_source, ("dp", "ctx"), split_axis=0, concat_axis=0, tiled=True)
        parts = returned.reshape(dp, ctx, ctx, piece_rows, Q_W)
        blocks = jnp.transpose(parts, (0, 2, 3, 1, 4))
    blocks = blocks.reshape(dev_count, piece_rows, HEADS * HEAD_DIM)
    return blocks[destinations].reshape(row_count, HEADS * HEAD_DIM)


def solution(mesh):
    return jax.shard_map(
        functools.partial(on_device, mesh.shape["dp"], mesh.shape["ctx"]),
        mesh=mesh,
        in_specs=(P(("dp", "ctx"), None), P("dp", None), P(("dp", "ctx"), None), P("dp", None)),
        out_specs=P(("dp", "ctx"), None),
        check_vma=False,
    )
```

```python
import functools
import math

import jax
import jax.numpy as jnp
from jax import lax
from jax.experimental import pallas as pl
from jax.experimental.pallas import tpu as pltpu
from jax.sharding import PartitionSpec as P

HEAD_DIM = 128
HEADS = 16
KV_HEADS = 4
GROUP = HEADS // KV_HEADS
Q_W = GROUP * HEAD_DIM
PART_W = Q_W + 2 * HEAD_DIM
MOST = 512
MESH = pl.DeviceIdType.MESH

theta_base = 500000.0


def position_tables(lengths, seq):
    position = jnp.arange(seq, dtype=jnp.int32)
    ends = jnp.cumsum(lengths)
    begins = jnp.max(
        jnp.where(position[:, None] >= ends[None, :], ends[None, :], 0), axis=1
    )
    half = HEAD_DIM // 2
    frequency = theta_base ** (-2.0 * jnp.arange(half, dtype=jnp.float32) / HEAD_DIM)
    angles = (position - begins).astype(jnp.float32)[:, None] * frequency[None, :]
    cosine, sine = jnp.cos(angles), jnp.sin(angles)
    return (
        jnp.concatenate([cosine, cosine], axis=1),
        jnp.concatenate([-sine, sine], axis=1),
        jnp.broadcast_to(begins[:, None].astype(jnp.float32), (seq, HEAD_DIM)),
    )


def attention_kernel(block, proj_ref, cos_ref, sin_ref, begin_ref, out_ref, key_ref):
    seq = proj_ref.shape[0]
    factor = HEAD_DIM**-0.5 * math.log2(math.e)

    def rotated(rows, column):
        x = proj_ref[rows, column : column + HEAD_DIM].astype(jnp.float32)
        turned = pltpu.roll(x, HEAD_DIM // 2, 1)
        return (x * cos_ref[rows, :] + turned * sin_ref[rows, :]).astype(jnp.bfloat16)

    for b in range(seq // block):
        rows = slice(b * block, (b + 1) * block)
        key_ref[rows, :] = rotated(rows, Q_W)
    for b in range(seq // block):
        rows = slice(b * block, (b + 1) * block)
        first = max(0, (b * block - (MOST - 1)) // block * block)
        keys = slice(first, (b + 1) * block)
        width = (b + 1) * block - first
        at = first + lax.broadcasted_iota(jnp.int32, (block, width), 1)
        own = b * block + lax.broadcasted_iota(jnp.int32, (block, width), 0)
        allowed = (at.astype(jnp.float32) >= begin_ref[rows, 0:1]) & (at <= own)
        values = proj_ref[keys, Q_W + HEAD_DIM : PART_W]
        for h in range(GROUP):
            scores = lax.dot_general(
                rotated(rows, h * HEAD_DIM),
                key_ref[keys, :],
                (((1,), (1,)), ((), ())),
                preferred_element_type=jnp.float32,
            )
            scores = jnp.where(allowed, scores, -jnp.inf)
            top = jnp.max(scores, axis=1, keepdims=True)
            weights = jnp.exp2((scores - top) * factor)
            total = jnp.sum(weights, axis=1, keepdims=True)
            mixed = jnp.dot(
                weights.astype(jnp.bfloat16), values, preferred_element_type=jnp.float32
            )
            out_ref[rows, h * HEAD_DIM : (h + 1) * HEAD_DIM] = (mixed / total).astype(jnp.bfloat16)


def attention(projected, lengths):
    seq = projected.shape[0]
    cosine, sine, begins = position_tables(lengths, seq)
    return pl.pallas_call(
        functools.partial(attention_kernel, 256),
        out_shape=jax.ShapeDtypeStruct((seq, Q_W), jnp.bfloat16),
        in_specs=[pl.BlockSpec(memory_space=pltpu.VMEM)] * 4,
        out_specs=pl.BlockSpec(memory_space=pltpu.VMEM),
        scratch_shapes=[pltpu.VMEM((seq, HEAD_DIM), jnp.bfloat16)],
        compiler_params=pltpu.CompilerParams(vmem_limit_bytes=32 * 2**20),
    )(projected, cosine, sine, begins)


PHASES = (
    ((HEADS * HEAD_DIM, HEAD_DIM, 0, HEAD_DIM), ((HEADS + KV_HEADS) * HEAD_DIM, HEAD_DIM, HEAD_DIM, HEAD_DIM),
     (0, Q_W, 2 * HEAD_DIM, Q_W // 2)),
    ((Q_W // 2, Q_W, 2 * HEAD_DIM + Q_W // 2, Q_W // 2),),
)
PHASE_COLUMNS = ((0, 2 * HEAD_DIM + Q_W // 2), (2 * HEAD_DIM + Q_W // 2, Q_W // 2))
RET_W = Q_W // 2


def whole_kernel(dp, ctx, chunk, slot_ref, len_ref, tok_ref, w_ref, ret_ref,
                 stage, ends, x_ref, w_buf, acc_ref, key_ref, val_ref, qry_ref, mix_ref, out_buf, tabs,
                 own_sem, wown_sem, tab_send, tab_recv, tok_send, tok_recv, z_send, z_recv,
                 c_send, c_recv, w_send, w_recv, f_send, f_recv, r_own, r_send, r_recv):
    d, c = lax.axis_index("dp"), lax.axis_index("ctx")
    devices = dp * ctx
    me = d * ctx + c
    dc, cz = d % 2, c % 2
    groups = devices // 4
    halves = ctx // 2
    s_me = (d // 2) * halves + c // 2
    m_me = dc * 2 + cz
    m_z = dc * 2 + 1 - cz
    d_sib, c_sib = d + 1 - 2 * dc, c + 1 - 2 * cz
    slab = groups * chunk
    depth = w_ref.shape[0]
    piece = chunk // ctx
    block = devices * piece
    seq = ctx * block

    def class_peer(s):
        return ((s // halves) * 2 + dc, (s % halves) * 2 + cz)

    def remote(src, dst, send, recv, device):
        return pltpu.make_async_remote_copy(
            src_ref=src, dst_ref=dst, send_sem=send, recv_sem=recv, device_id=device, device_id_type=MESH
        )

    barrier = pltpu.get_barrier_semaphore()

    @pl.loop(1, devices)
    def _(t):
        other = (me + t) % devices
        pl.semaphore_signal(barrier, inc=1, device_id=(other // ctx, other % ctx), device_id_type=MESH)

    @pl.loop(0, devices // 2, unroll=4)
    def _(pair):
        both = [tok_ref[slot_ref[pair * 2 + i]] for i in range(2)]
        stage[pl.ds(pl.multiple_of(pair * 2 * piece, 2 * piece), 2 * piece), :] = jnp.concatenate(both, axis=0)

    document = lax.broadcasted_iota(jnp.int32, ends.shape[1:], 0)
    end, table = jnp.int32(0), jnp.zeros(ends.shape[1:], jnp.int32)
    for j in range(ends.shape[1]):
        end = end + len_ref[0, j]
        table = jnp.where(document == j, end, table)
    ends[dc] = table

    pl.semaphore_wait(barrier, devices - 1)

    def x_rows(m, s):
        return x_ref.at[pl.ds(pl.multiple_of(m * slab + s * chunk, chunk), chunk), :]

    def tok_rows(s):
        return stage.at[pl.ds(pl.multiple_of(s * chunk, chunk), chunk), :]

    own = pltpu.make_async_copy(tok_rows(s_me), x_rows(m_me, s_me), own_sem)

    def tok_copy(t):
        s = (s_me + t) % groups
        return remote(tok_rows(s), x_rows(m_me, s_me), tok_send.at[t], tok_recv.at[t], class_peer(s))

    tab_out = remote(ends.at[dc], ends.at[dc], tab_send, tab_recv, (d_sib, c))
    tab_in = remote(ends.at[1 - dc], ends.at[1 - dc], tab_send, tab_recv, (d_sib, c))

    chip = d // 2
    chip_x = chip + 1 - 2 * (chip % 2)
    chip_y = (chip + 2) % 4
    chip_far = (chip_x + 2) % 4

    def w_parts(d_to, d_from, phase):
        g = (d_to % 2) * 2 + cz
        for i, (base, stride, to, width) in enumerate(PHASES[phase]):
            start = pl.multiple_of(base + g * stride, HEAD_DIM)
            yield (w_ref.at[:, pl.ds(start, width)], w_buf.at[d_from, :, to : to + width], 3 * phase + i)

    near = ((0, d_sib), (1, chip_x * 2 + dc), (2, chip_x * 2 + 1 - dc), (3, chip_y * 2 + dc), (4, chip_y * 2 + 1 - dc))

    def w_out(phase, slots=range(5)):
        return [remote(src, dst, w_send.at[slot, i], w_recv.at[slot, i], (d_to, c))
                for slot, d_to in near if slot in slots for src, dst, i in w_parts(d_to, d, phase)]

    def w_in(phase, slots):
        return [remote(src, dst, w_send.at[slot, i], w_recv.at[slot, i], (d_from, c))
                for slot, d_from in near if slot in slots for src, dst, i in w_parts(d, d_from, phase)]

    w_own = [pltpu.make_async_copy(src, dst, wown_sem.at[i])
             for phase in range(2) for src, dst, i in w_parts(d, d, phase)]

    half = depth // 2

    def f_parts(chip_from, way, phase, chip_to):
        for core in range(2):
            for i, (_, _, to, width) in enumerate(PHASES[phase]):
                there = w_buf.at[chip_from * 2 + core, way * half : (way + 1) * half, to : to + width]
                yield remote(there, there, f_send.at[way, core, 3 * phase + i], f_recv.at[way, core, 3 * phase + i],
                             (chip_to * 2 + dc, c))

    def f_out(phase, way):
        return list(f_parts((chip_x, chip_y)[way], way, phase, (chip_y, chip_x)[way]))

    def f_in(phase, way):
        return list(f_parts(chip_far, way, phase, (chip_y, chip_x)[way]))

    def came(t):
        return (s_me - t + groups) % groups

    def z_copy(t):
        at = x_rows(m_me, came(t)) if t else tok_rows(s_me)
        return remote(at, x_rows(m_me, came(t)), z_send.at[t], z_recv.at[t], (d, c_sib))

    def z_arrival(t):
        return remote(x_rows(m_z, came(t)), x_rows(m_z, came(t)), z_send.at[t], z_recv.at[t], (d, c_sib))

    def c_copy(which, t):
        to = x_rows(m_z if which else m_me, came(t))
        at = to if t or which else tok_rows(s_me)
        return remote(at, to, c_send.at[which, t], c_recv.at[which, t], (d_sib, c))

    def c_arrival(which, t):
        at = x_rows((1 - dc) * 2 + (1 - cz if which else cz), came(t))
        return remote(at, at, c_send.at[which, t], c_recv.at[which, t], (d_sib, c))

    z_copy(0).start()
    for t in range(1, groups):
        tok_copy(t).start()
        for copy in w_out(0, (t,) if t < 5 else ()):
            copy.start()
    tab_out.start()
    c_copy(0, 0).start()
    for copy in w_out(0, (0,)):
        copy.start()
    own.start()
    for copy in w_own:
        copy.start()

    tab_in.wait_recv()

    @pl.loop(0, seq // 64)
    def _(n):
        rows = pl.ds(pl.multiple_of(n * 64, 64), 64)
        position = n * 64 + lax.broadcasted_iota(jnp.int32, (64, HEAD_DIM), 0)
        lane = lax.broadcasted_iota(jnp.int32, (1, HEAD_DIM), 1)
        begin = jnp.zeros((64, HEAD_DIM), jnp.int32)
        for j in range(ends.shape[1]):
            end = ends[c // 2, j : j + 1, :]
            begin = jnp.maximum(begin, jnp.where(position >= end, end, 0))
        spread = (lane % (HEAD_DIM // 2)).astype(jnp.float32) * (-2.0 * math.log(theta_base) / HEAD_DIM)
        angles = (position - begin).astype(jnp.float32) * jnp.exp(spread)
        sine = jnp.sin(angles)
        tabs[0, rows, :] = jnp.cos(angles)
        tabs[1, rows, :] = jnp.where(lane < HEAD_DIM // 2, -sine, sine)
        tabs[2, rows, :] = begin.astype(jnp.float32)

    for t in range(1, groups):
        remote(tok_rows(came(t)), x_rows(m_me, came(t)), tok_send.at[t], tok_recv.at[t],
               class_peer(came(t))).wait_recv()
        z_copy(t).start()
        c_copy(0, t).start()
    for copy in w_out(1):
        copy.start()

    def forward_weights(phase):
        for way in range(2):
            for copy in w_in(phase, ((1, 2), (3, 4))[way]):
                copy.wait_recv()
            for copy in f_out(phase, way):
                copy.start()

    for t in range(groups):
        if t == groups // 2:
            forward_weights(0)
        z_arrival(t).wait_recv()
        c_copy(1, t).start()
    forward_weights(1)

    def multiply(m, phase):
        rows = pl.ds(pl.multiple_of(m * slab, slab), slab)
        first, width = PHASE_COLUMNS[phase]

        def product(k):
            columns = pl.ds(pl.multiple_of(k * depth, depth), depth)
            return jnp.dot(x_ref[rows, columns], w_buf[k, :, first : first + width],
                           preferred_element_type=jnp.float32)

        acc_ref[rows, 0:width] = product(0)

        @pl.loop(1, dp)
        def _(k):
            acc_ref[rows, 0:width] += product(k)

    def rows_of(i, q, first, width):
        src_d, src_c = i // ctx, i % ctx
        m = (src_d % 2) * 2 + src_c % 2
        s = (src_d // 2) * halves + src_c // 2
        start = pl.multiple_of(m * slab + s * chunk + q * piece, piece)
        return acc_ref[pl.ds(start, piece), first : first + width]

    def rotate(x, at):
        x = x.astype(jnp.bfloat16).astype(jnp.float32)
        turned = pltpu.roll(x, HEAD_DIM // 2, 1)
        cosine = tabs[0, pl.ds(at, 2 * piece), :]
        sine = tabs[1, pl.ds(at, 2 * piece), :]
        return (x * cosine + turned * sine).astype(jnp.bfloat16)

    def pack(phase):
        @pl.loop(0, devices // 2, unroll=2)
        def _(pair):
            for q in range(ctx):
                def both(first):
                    return jnp.concatenate(
                        [rows_of(pair * 2 + i, q, first, HEAD_DIM) for i in range(2)], axis=0)

                at = pl.multiple_of(q * block + pair * 2 * piece, 2 * piece)
                to = pl.ds(at, 2 * piece)
                if phase == 0:
                    key_ref[to, :] = rotate(both(0), at)
                    val_ref[to, :] = both(HEAD_DIM).astype(jnp.bfloat16)
                base = 2 * HEAD_DIM if phase == 0 else 0
                for h in range(GROUP // 2):
                    qry_ref[to, h * HEAD_DIM : (h + 1) * HEAD_DIM] = rotate(both(base + h * HEAD_DIM), at)

    factor = HEAD_DIM**-0.5 * math.log2(math.e)

    def attend():
        for b in range(ctx):
            rows = slice(b * block, (b + 1) * block)
            first = max(0, (b * block - (MOST - 1)) // block * block)
            keys = slice(first, (b + 1) * block)
            width = (b + 1) * block - first
            at = first + lax.broadcasted_iota(jnp.int32, (block, width), 1)
            at_own = b * block + lax.broadcasted_iota(jnp.int32, (block, width), 0)
            begin = tabs[2, rows, 0:1]
            allowed = (at.astype(jnp.float32) >= begin) & (at <= at_own)
            for h in range(GROUP // 2):
                scores = lax.dot_general(
                    qry_ref[rows, h * HEAD_DIM : (h + 1) * HEAD_DIM], key_ref[keys, :],
                    (((1,), (1,)), ((), ())), preferred_element_type=jnp.float32,
                )
                scores = jnp.where(allowed, scores, -jnp.inf)
                top = jnp.max(scores, axis=1, keepdims=True)
                weights = jnp.exp2((scores - top) * factor)
                total = jnp.sum(weights, axis=1, keepdims=True)
                mixed = jnp.dot(weights.astype(jnp.bfloat16), val_ref[keys, :],
                                preferred_element_type=jnp.float32)
                mix_ref[rows, h * HEAD_DIM : (h + 1) * HEAD_DIM] = mixed / total

    def ret_at(s, m, phase):
        return ret_ref.at[pl.ds(pl.multiple_of(s * chunk, chunk), chunk),
                          pl.ds(pl.multiple_of(m * Q_W + phase * RET_W, RET_W), RET_W)]

    def buf_at(i, phase):
        return out_buf.at[phase, pl.ds(pl.multiple_of(i * chunk, chunk), chunk), :]

    def ret_copy(phase, t):
        i = (me + t) % devices
        return remote(buf_at(i, phase), ret_at(s_me, m_me, phase), r_send.at[phase, t], r_recv.at[phase, t],
                      (i // ctx, i % ctx))

    def ret_arrival(phase, t):
        i = (me - t + devices) % devices
        src_d, src_c = i // ctx, i % ctx
        s = (src_d // 2) * halves + src_c // 2
        m = (src_d % 2) * 2 + src_c % 2
        return remote(buf_at(i, phase), ret_at(s, m, phase), r_send.at[phase, t], r_recv.at[phase, t],
                      (src_d, src_c))

    def own_ret(phase):
        return pltpu.make_async_copy(buf_at(me, phase), ret_at(s_me, m_me, phase), r_own.at[phase])

    def send_back(phase):
        def ready(i):
            parts = [mix_ref[pl.ds(pl.multiple_of(q * block + i * piece, piece), piece), :] for q in range(ctx)]
            out_buf[phase, pl.ds(pl.multiple_of(i * chunk, chunk), chunk), :] = (
                jnp.concatenate(parts, axis=0).astype(jnp.bfloat16))

        @pl.loop(1, devices)
        def _(t):
            ready((me + t) % devices)
            ret_copy(phase, t).start()

        ready(me)
        own_ret(phase).start()

    own.wait()
    for copy in w_own:
        copy.wait()
    for phase in range(2):
        for copy in w_in(phase, (0,)) + f_in(phase, 0) + f_in(phase, 1):
            copy.wait_recv()
        multiply(m_me, phase)
        multiply(m_z, phase)
        for which in range(2):
            if phase == 0:
                for t in range(groups):
                    c_arrival(which, t).wait_recv()
            multiply((1 - dc) * 2 + (1 - cz if which else cz), phase)
        pack(phase)
        attend()
        send_back(phase)

    tab_out.wait_send()
    for t in range(groups):
        if t > 0:
            tok_copy(t).wait_send()
        z_copy(t).wait_send()
        c_copy(0, t).wait_send()
        c_copy(1, t).wait_send()
    for phase in range(2):
        for copy in w_out(phase) + f_out(phase, 0) + f_out(phase, 1):
            copy.wait_send()
        own_ret(phase).wait()

        @pl.loop(1, devices)
        def _(t):
            ret_copy(phase, t).wait_send()
            ret_arrival(phase, t).wait_recv()


def attended_blocks(slot_of, lengths, tokens, weights, dp, ctx):
    devices, piece, width = tokens.shape
    rows = devices * piece
    depth = weights.shape[0]
    groups = devices // 4
    chunk = rows // groups
    seq = 4 * rows
    dma = pltpu.SemaphoreType.DMA
    return pl.pallas_call(
        functools.partial(whole_kernel, dp, ctx, chunk),
        out_shape=jax.ShapeDtypeStruct((rows, HEADS * HEAD_DIM), jnp.bfloat16),
        in_specs=[
            pl.BlockSpec(memory_space=pltpu.SMEM),
            pl.BlockSpec(memory_space=pltpu.SMEM),
            pl.BlockSpec(memory_space=pltpu.VMEM),
            pl.BlockSpec(memory_space=pl.ANY),
        ],
        out_specs=pl.BlockSpec(memory_space=pl.ANY),
        scratch_shapes=[
            pltpu.VMEM((rows, width), jnp.bfloat16),
            pltpu.VMEM((2, lengths.shape[1], HEAD_DIM), jnp.int32),
            pltpu.VMEM((seq, width), jnp.bfloat16),
            pltpu.VMEM((dp, depth, PART_W), jnp.bfloat16),
            pltpu.VMEM((seq, PHASE_COLUMNS[0][1]), jnp.float32),
            pltpu.VMEM((seq, HEAD_DIM), jnp.bfloat16),
            pltpu.VMEM((seq, HEAD_DIM), jnp.bfloat16),
            pltpu.VMEM((seq, RET_W), jnp.bfloat16),
            pltpu.VMEM((seq, RET_W), jnp.float32),
            pltpu.VMEM((2, seq, RET_W), jnp.bfloat16),
            pltpu.VMEM((3, seq, HEAD_DIM), jnp.float32),
            dma, dma((4,)), dma, dma,
            dma((groups,)), dma((groups,)),
            dma((groups,)), dma((groups,)),
            dma((2, groups)), dma((2, groups)),
            dma((5, 4)), dma((5, 4)),
            dma((2, 2, 4)), dma((2, 2, 4)),
            dma((2,)), dma((2, devices)), dma((2, devices)),
        ],
        compiler_params=pltpu.CompilerParams(
            collective_id=0, has_side_effects=True, vmem_limit_bytes=48 * 2**20
        ),
    )(slot_of, lengths, tokens, weights)


def on_device(dp, ctx, tokens, projection, placement, doc_lengths):
    row_count, width = tokens.shape
    dev_count = placement.shape[1]
    piece_rows = row_count // dev_count
    destinations = placement[0]
    index = jnp.arange(dev_count, dtype=jnp.int32)
    slot_of = jnp.sum(jnp.where(destinations[None, :] == index[:, None], index[None, :], 0), axis=1)
    pieces = tokens.reshape(dev_count, piece_rows, width)
    if dp == 8 and ctx == 4 and piece_rows == 8:
        blocks = attended_blocks(slot_of, doc_lengths, pieces, projection, dp, ctx)
    else:
        c = lax.axis_index("ctx")
        arrived = lax.all_to_all(pieces[slot_of], ("dp", "ctx"), split_axis=0, concat_axis=0, tiled=True)
        rows = lax.all_gather(arrived.reshape(row_count, width), "ctx", axis=0, tiled=True)
        cuts = [
            lax.dynamic_slice_in_dim(projection, base + c * w, w, axis=1)
            for base, w in ((0, Q_W), (HEADS * HEAD_DIM, HEAD_DIM), ((HEADS + KV_HEADS) * HEAD_DIM, HEAD_DIM))
        ]
        weights = lax.all_gather(jnp.concatenate(cuts, axis=1), "dp", axis=0, tiled=True)
        projected = jnp.dot(rows, weights, preferred_element_type=jnp.float32).astype(jnp.bfloat16)
        mixed = attention(projected, doc_lengths[0])
        by_source = jnp.transpose(mixed.reshape(ctx, dev_count, piece_rows, Q_W), (1, 0, 2, 3))
        returned = lax.all_to_all(by_source, ("dp", "ctx"), split_axis=0, concat_axis=0, tiled=True)
        parts = returned.reshape(dp, ctx, ctx, piece_rows, Q_W)
        blocks = jnp.transpose(parts, (0, 2, 3, 1, 4))
    blocks = blocks.reshape(dev_count, piece_rows, HEADS * HEAD_DIM)
    return blocks[destinations].reshape(row_count, HEADS * HEAD_DIM)


def solution(mesh):
    return jax.shard_map(
        functools.partial(on_device, mesh.shape["dp"], mesh.shape["ctx"]),
        mesh=mesh,
        in_specs=(P(("dp", "ctx"), None), P("dp", None), P(("dp", "ctx"), None), P("dp", None)),
        out_specs=P(("dp", "ctx"), None),
        check_vma=False,
    )
```

```python
import functools
import math

import jax
import jax.numpy as jnp
from jax import lax
from jax.experimental import pallas as pl
from jax.experimental.pallas import tpu as pltpu
from jax.sharding import PartitionSpec as P

HEAD_DIM = 128
HEADS = 16
KV_HEADS = 4
GROUP = HEADS // KV_HEADS
Q_W = GROUP * HEAD_DIM
PART_W = Q_W + 2 * HEAD_DIM
MOST = 512
MESH = pl.DeviceIdType.MESH

theta_base = 500000.0


def position_tables(lengths, seq):
    position = jnp.arange(seq, dtype=jnp.int32)
    ends = jnp.cumsum(lengths)
    begins = jnp.max(
        jnp.where(position[:, None] >= ends[None, :], ends[None, :], 0), axis=1
    )
    half = HEAD_DIM // 2
    frequency = theta_base ** (-2.0 * jnp.arange(half, dtype=jnp.float32) / HEAD_DIM)
    angles = (position - begins).astype(jnp.float32)[:, None] * frequency[None, :]
    cosine, sine = jnp.cos(angles), jnp.sin(angles)
    return (
        jnp.concatenate([cosine, cosine], axis=1),
        jnp.concatenate([-sine, sine], axis=1),
        jnp.broadcast_to(begins[:, None].astype(jnp.float32), (seq, HEAD_DIM)),
    )


def attention_kernel(block, proj_ref, cos_ref, sin_ref, begin_ref, out_ref, key_ref):
    seq = proj_ref.shape[0]
    factor = HEAD_DIM**-0.5 * math.log2(math.e)

    def rotated(rows, column):
        x = proj_ref[rows, column : column + HEAD_DIM].astype(jnp.float32)
        turned = pltpu.roll(x, HEAD_DIM // 2, 1)
        return (x * cos_ref[rows, :] + turned * sin_ref[rows, :]).astype(jnp.bfloat16)

    for b in range(seq // block):
        rows = slice(b * block, (b + 1) * block)
        key_ref[rows, :] = rotated(rows, Q_W)
    for b in range(seq // block):
        rows = slice(b * block, (b + 1) * block)
        first = max(0, (b * block - (MOST - 1)) // block * block)
        keys = slice(first, (b + 1) * block)
        width = (b + 1) * block - first
        at = first + lax.broadcasted_iota(jnp.int32, (block, width), 1)
        own = b * block + lax.broadcasted_iota(jnp.int32, (block, width), 0)
        allowed = (at.astype(jnp.float32) >= begin_ref[rows, 0:1]) & (at <= own)
        values = proj_ref[keys, Q_W + HEAD_DIM : PART_W]
        for h in range(GROUP):
            scores = lax.dot_general(
                rotated(rows, h * HEAD_DIM),
                key_ref[keys, :],
                (((1,), (1,)), ((), ())),
                preferred_element_type=jnp.float32,
            )
            scores = jnp.where(allowed, scores, -jnp.inf)
            top = jnp.max(scores, axis=1, keepdims=True)
            weights = jnp.exp2((scores - top) * factor)
            total = jnp.sum(weights, axis=1, keepdims=True)
            mixed = jnp.dot(
                weights.astype(jnp.bfloat16), values, preferred_element_type=jnp.float32
            )
            out_ref[rows, h * HEAD_DIM : (h + 1) * HEAD_DIM] = (mixed / total).astype(jnp.bfloat16)


def attention(projected, lengths):
    seq = projected.shape[0]
    cosine, sine, begins = position_tables(lengths, seq)
    return pl.pallas_call(
        functools.partial(attention_kernel, 256),
        out_shape=jax.ShapeDtypeStruct((seq, Q_W), jnp.bfloat16),
        in_specs=[pl.BlockSpec(memory_space=pltpu.VMEM)] * 4,
        out_specs=pl.BlockSpec(memory_space=pltpu.VMEM),
        scratch_shapes=[pltpu.VMEM((seq, HEAD_DIM), jnp.bfloat16)],
        compiler_params=pltpu.CompilerParams(vmem_limit_bytes=32 * 2**20),
    )(projected, cosine, sine, begins)


PHASES = (
    ((HEADS * HEAD_DIM, HEAD_DIM, 0, HEAD_DIM), ((HEADS + KV_HEADS) * HEAD_DIM, HEAD_DIM, HEAD_DIM, HEAD_DIM),
     (0, Q_W, 2 * HEAD_DIM, Q_W // 2)),
    ((Q_W // 2, Q_W, 2 * HEAD_DIM + Q_W // 2, Q_W // 2),),
)

def whole_kernel(dp, ctx, chunk, slot_ref, len_ref, tok_hbm, w_ref, ret_ref,
                 tok_ref, stage, ends, x_ref, w_buf, acc_ref, key_ref, val_ref, qry_ref, mix_ref, out_buf, tabs,
                 in_sem, own_sem, wown_sem, tab_send, tab_recv, tok_send, tok_recv, z_send, z_recv,
                 c_send, c_recv, w_send, w_recv, f_send, f_recv, r_own, r_send, r_recv):
    d, c = lax.axis_index("dp"), lax.axis_index("ctx")
    devices = dp * ctx
    me = d * ctx + c
    dc, cz = d % 2, c % 2
    groups = devices // 4
    halves = ctx // 2
    s_me = (d // 2) * halves + c // 2
    m_me = dc * 2 + cz
    m_z = dc * 2 + 1 - cz
    d_sib, c_sib = d + 1 - 2 * dc, c + 1 - 2 * cz
    part = chunk // 2
    slab = groups * part
    depth = w_ref.shape[0]
    piece = chunk // ctx
    block = devices * piece
    seq = ctx * block
    rows_half = seq // 2
    quarters = ctx // 2

    def class_peer(s):
        return ((s // halves) * 2 + dc, (s % halves) * 2 + cz)

    def remote(src, dst, send, recv, device):
        return pltpu.make_async_remote_copy(
            src_ref=src, dst_ref=dst, send_sem=send, recv_sem=recv, device_id=device, device_id_type=MESH
        )

    tok_in = pltpu.make_async_copy(tok_hbm, tok_ref, in_sem)
    tok_in.start()

    barrier = pltpu.get_barrier_semaphore()

    @pl.loop(1, devices)
    def _(t):
        other = (me + t) % devices
        pl.semaphore_signal(barrier, inc=1, device_id=(other // ctx, other % ctx), device_id_type=MESH)

    document = lax.broadcasted_iota(jnp.int32, ends.shape[1:], 0)
    end, table = jnp.int32(0), jnp.zeros(ends.shape[1:], jnp.int32)
    for j in range(ends.shape[1]):
        end = end + len_ref[0, j]
        table = jnp.where(document == j, end, table)
    ends[dc] = table

    pl.semaphore_wait(barrier, devices - 1)

    def gather(s, h):
        at = s * ctx + h * quarters
        rows = [tok_ref[slot_ref[at + q]] for q in range(quarters)]
        start = pl.multiple_of(s * chunk + h * part, part)
        stage[pl.ds(start, part), :] = jnp.concatenate(rows, axis=0)

    def x_rows(m, s, h):
        return x_ref.at[pl.ds(pl.multiple_of(h * rows_half + m * slab + s * part, part), part), :]

    def tok_rows(s, h):
        return stage.at[pl.ds(pl.multiple_of(s * chunk + h * part, part), part), :]

    def own_copy(h):
        return pltpu.make_async_copy(tok_rows(s_me, h), x_rows(m_me, s_me, h), own_sem.at[h])

    def tok_copy(t, h):
        s = (s_me + t) % groups
        return remote(tok_rows(s, h), x_rows(m_me, s_me, h), tok_send.at[h, t], tok_recv.at[h, t], class_peer(s))

    tab_out = remote(ends.at[dc], ends.at[dc], tab_send, tab_recv, (d_sib, c))
    tab_in = remote(ends.at[1 - dc], ends.at[1 - dc], tab_send, tab_recv, (d_sib, c))

    chip = d // 2
    chip_x = chip + 1 - 2 * (chip % 2)
    chip_y = (chip + 2) % 4
    chip_far = (chip_x + 2) % 4

    def w_parts(d_to, d_from, phase):
        g = (d_to % 2) * 2 + cz
        for i, (base, stride, to, width) in enumerate(PHASES[phase]):
            start = pl.multiple_of(base + g * stride, HEAD_DIM)
            yield (w_ref.at[:, pl.ds(start, width)], w_buf.at[d_from, :, to : to + width], 3 * phase + i)

    near = ((0, d_sib), (1, chip_x * 2 + dc), (2, chip_x * 2 + 1 - dc), (3, chip_y * 2 + dc), (4, chip_y * 2 + 1 - dc))

    def w_out(phase, slots=range(5)):
        return [remote(src, dst, w_send.at[slot, i], w_recv.at[slot, i], (d_to, c))
                for slot, d_to in near if slot in slots for src, dst, i in w_parts(d_to, d, phase)]

    def w_in(phase, slots):
        return [remote(src, dst, w_send.at[slot, i], w_recv.at[slot, i], (d_from, c))
                for slot, d_from in near if slot in slots for src, dst, i in w_parts(d, d_from, phase)]

    w_own = [pltpu.make_async_copy(src, dst, wown_sem.at[i])
             for phase in range(2) for src, dst, i in w_parts(d, d, phase)]

    half = depth // 2

    def f_parts(chip_from, way, phase, chip_to):
        for core in range(2):
            for i, (_, _, to, width) in enumerate(PHASES[phase]):
                there = w_buf.at[chip_from * 2 + core, way * half : (way + 1) * half, to : to + width]
                yield remote(there, there, f_send.at[way, core, 3 * phase + i], f_recv.at[way, core, 3 * phase + i],
                             (chip_to * 2 + dc, c))

    def f_out(phase, way):
        return list(f_parts((chip_x, chip_y)[way], way, phase, (chip_y, chip_x)[way]))

    def f_in(phase, way):
        return list(f_parts(chip_far, way, phase, (chip_y, chip_x)[way]))

    def came(t):
        return (s_me - t + groups) % groups

    def tok_arrival(t, h):
        return remote(tok_rows(came(t), h), x_rows(m_me, came(t), h), tok_send.at[h, t], tok_recv.at[h, t],
                      class_peer(came(t)))

    def z_copy(t, h):
        to = x_rows(m_me, came(t), h)
        at = to if t else tok_rows(s_me, h)
        return remote(at, to, z_send.at[h, t], z_recv.at[h, t], (d, c_sib))

    def z_arrival(t, h):
        at = x_rows(m_z, came(t), h)
        return remote(at, at, z_send.at[h, t], z_recv.at[h, t], (d, c_sib))

    def c_copy(which, t, h):
        to = x_rows(m_z if which else m_me, came(t), h)
        at = to if t or which else tok_rows(s_me, h)
        return remote(at, to, c_send.at[h, which, t], c_recv.at[h, which, t], (d_sib, c))

    def c_arrival(which, t, h):
        at = x_rows((1 - dc) * 2 + (1 - cz if which else cz), came(t), h)
        return remote(at, at, c_send.at[h, which, t], c_recv.at[h, which, t], (d_sib, c))

    def forward_class(h, ts):
        for t in ts:
            tok_arrival(t, h).wait_recv()
            z_copy(t, h).start()
            c_copy(0, t, h).start()

    def forward_z(h, ts):
        for t in ts:
            z_arrival(t, h).wait_recv()
            c_copy(1, t, h).start()

    def start_own(h):
        gather(s_me, h)
        z_copy(0, h).start()
        c_copy(0, 0, h).start()
        own_copy(h).start()

    tab_out.start()
    tok_in.wait()
    for t in range(1, groups):
        gather((s_me + t) % groups, 0)
        tok_copy(t, 0).start()
        if t == 1:
            start_own(0)
        for copy in w_out(0, (t,) if t < 5 else ()):
            copy.start()
    for copy in w_out(0, (0,)) + w_out(1):
        copy.start()
    for copy in w_own:
        copy.start()

    for t in range(1, groups):
        gather((s_me + t) % groups, 1)
    forward_class(0, range(1, groups))
    for t in range(1, groups):
        tok_copy(t, 1).start()
    start_own(1)

    tab_in.wait_recv()

    @pl.loop(0, seq // 64)
    def _(n):
        rows = pl.ds(pl.multiple_of(n * 64, 64), 64)
        position = n * 64 + lax.broadcasted_iota(jnp.int32, (64, HEAD_DIM), 0)
        lane = lax.broadcasted_iota(jnp.int32, (1, HEAD_DIM), 1)
        begin = jnp.zeros((64, HEAD_DIM), jnp.int32)
        for j in range(ends.shape[1]):
            end = ends[c // 2, j : j + 1, :]
            begin = jnp.maximum(begin, jnp.where(position >= end, end, 0))
        spread = (lane % (HEAD_DIM // 2)).astype(jnp.float32) * (-2.0 * math.log(theta_base) / HEAD_DIM)
        angles = (position - begin).astype(jnp.float32) * jnp.exp(spread)
        sine = jnp.sin(angles)
        tabs[0, rows, :] = jnp.cos(angles)
        tabs[1, rows, :] = jnp.where(lane < HEAD_DIM // 2, -sine, sine)
        tabs[2, rows, :] = begin.astype(jnp.float32)

    def forward_weights(phase):
        for way in range(2):
            for copy in w_in(phase, ((1, 2), (3, 4))[way]):
                copy.wait_recv()
            for copy in f_out(phase, way):
                copy.start()

    forward_z(0, range(groups // 2))
    forward_weights(0)
    forward_z(0, range(groups // 2, groups))
    forward_class(1, range(1, groups))
    forward_weights(1)

    def rows_of(i, q, first):
        src_d, src_c = i // ctx, i % ctx
        m = (src_d % 2) * 2 + src_c % 2
        s = (src_d // 2) * halves + src_c // 2
        start = pl.multiple_of(m * slab + s * part + q * piece, piece)
        return acc_ref[pl.ds(start, piece), first : first + HEAD_DIM]

    def rotate(x, at):
        x = x.astype(jnp.bfloat16).astype(jnp.float32)
        turned = pltpu.roll(x, HEAD_DIM // 2, 1)
        cosine = tabs[0, pl.ds(at, 2 * piece), :]
        sine = tabs[1, pl.ds(at, 2 * piece), :]
        return (x * cosine + turned * sine).astype(jnp.bfloat16)

    def pack(half_at):
        @pl.loop(0, devices // 2, unroll=2)
        def _(pair):
            for q in range(quarters):
                def both(first):
                    return jnp.concatenate([rows_of(pair * 2 + i, q, first) for i in range(2)], axis=0)

                near_at = pl.multiple_of(q * block + pair * 2 * piece, 2 * piece)
                at = pl.multiple_of(half_at * rows_half + near_at, 2 * piece)
                to = pl.ds(at, 2 * piece)
                key_ref[to, :] = rotate(both(0), at)
                val_ref[to, :] = both(HEAD_DIM).astype(jnp.bfloat16)
                for h in range(GROUP):
                    qry_ref[pl.ds(near_at, 2 * piece), h * HEAD_DIM : (h + 1) * HEAD_DIM] = rotate(
                        both((2 + h) * HEAD_DIM), at)

    factor = HEAD_DIM**-0.5 * math.log2(math.e)

    def attend(half_at):
        for j in range(quarters):
            b = half_at * quarters + j
            rows = slice(b * block, (b + 1) * block)
            near_rows = slice(j * block, (j + 1) * block)
            first = max(0, (b * block - (MOST - 1)) // block * block)
            keys = slice(first, (b + 1) * block)
            width = (b + 1) * block - first
            at = first + lax.broadcasted_iota(jnp.int32, (block, width), 1)
            at_own = b * block + lax.broadcasted_iota(jnp.int32, (block, width), 0)
            begin = tabs[2, rows, 0:1]
            allowed = (at.astype(jnp.float32) >= begin) & (at <= at_own)
            for h in range(GROUP):
                scores = lax.dot_general(
                    qry_ref[near_rows, h * HEAD_DIM : (h + 1) * HEAD_DIM], key_ref[keys, :],
                    (((1,), (1,)), ((), ())), preferred_element_type=jnp.float32,
                )
                scores = jnp.where(allowed, scores, -jnp.inf)
                top = jnp.max(scores, axis=1, keepdims=True)
                weights = jnp.exp2((scores - top) * factor)
                total = jnp.sum(weights, axis=1, keepdims=True)
                mixed = jnp.dot(weights.astype(jnp.bfloat16), val_ref[keys, :],
                                preferred_element_type=jnp.float32)
                mix_ref[near_rows, h * HEAD_DIM : (h + 1) * HEAD_DIM] = mixed / total

    def ret_at(s, m, h):
        return ret_ref.at[pl.ds(pl.multiple_of(s * chunk + h * part, part), part),
                          pl.ds(pl.multiple_of(m * Q_W, Q_W), Q_W)]

    def buf_at(i, h):
        return out_buf.at[h, pl.ds(pl.multiple_of(i * part, part), part), :]

    def ret_copy(h, t):
        i = (me + t) % devices
        return remote(buf_at(i, h), ret_at(s_me, m_me, h), r_send.at[h, t], r_recv.at[h, t], (i // ctx, i % ctx))

    def ret_arrival(h, t):
        i = (me - t + devices) % devices
        src_d, src_c = i // ctx, i % ctx
        s = (src_d // 2) * halves + src_c // 2
        m = (src_d % 2) * 2 + src_c % 2
        return remote(buf_at(i, h), ret_at(s, m, h), r_send.at[h, t], r_recv.at[h, t], (src_d, src_c))

    def own_ret(h):
        return pltpu.make_async_copy(buf_at(me, h), ret_at(s_me, m_me, h), r_own.at[h])

    def send_back(h):
        def ready(i):
            parts = [mix_ref[pl.ds(pl.multiple_of(q * block + i * piece, piece), piece), :] for q in range(quarters)]
            out_buf[h, pl.ds(pl.multiple_of(i * part, part), part), :] = (
                jnp.concatenate(parts, axis=0).astype(jnp.bfloat16))

        @pl.loop(1, devices)
        def _(t):
            ready((me + t) % devices)
            ret_copy(h, t).start()

        ready(me)
        own_ret(h).start()

    own_copy(0).wait()
    for t in range(groups):
        for which in range(2):
            c_arrival(which, t, 0).wait_recv()
    for copy in w_own:
        copy.wait()

    def multiply(rows, k, start, extent):
        columns = pl.ds(pl.multiple_of(k * depth + start, extent), extent)
        return jnp.dot(x_ref[rows, columns], w_buf[k, start : start + extent, :],
                       preferred_element_type=jnp.float32)

    early = pl.ds(0, rows_half)
    acc_ref[...] = multiply(early, d, 0, depth)
    for copy in w_in(0, (0,)) + w_in(1, (0,)):
        copy.wait_recv()
    for _, d_from in near:
        acc_ref[...] += multiply(early, d_from, 0, depth)
    for way in range(2):
        for copy in f_in(0, way) + f_in(1, way):
            copy.wait_recv()
        for core in range(2):
            acc_ref[...] += multiply(early, chip_far * 2 + core, way * half, half)
    forward_z(1, range(groups // 2))
    pack(0)
    attend(0)
    send_back(0)

    forward_z(1, range(groups // 2, groups))
    own_copy(1).wait()
    for which in range(2):
        if which:
            for t in range(groups):
                c_arrival(0, t, 1).wait_recv()
                c_arrival(1, t, 1).wait_recv()
        base = (1 - dc if which else dc) * 2 * slab
        to = pl.ds(pl.multiple_of(base, 2 * slab), 2 * slab)
        rows = pl.ds(pl.multiple_of(rows_half + base, 2 * slab), 2 * slab)
        acc_ref[to, :] = multiply(rows, 0, 0, depth)

        @pl.loop(1, dp)
        def _(k):
            acc_ref[to, :] += multiply(rows, k, 0, depth)

    pack(1)
    attend(1)
    send_back(1)

    tab_out.wait_send()
    for copy in w_out(0) + w_out(1) + [copy for way in range(2) for phase in range(2) for copy in f_out(phase, way)]:
        copy.wait_send()
    for h in range(2):
        for t in range(groups):
            if t > 0:
                tok_copy(t, h).wait_send()
            z_copy(t, h).wait_send()
            c_copy(0, t, h).wait_send()
            c_copy(1, t, h).wait_send()
        own_ret(h).wait()

        @pl.loop(1, devices)
        def _(t):
            ret_copy(h, t).wait_send()
            ret_arrival(h, t).wait_recv()


def attended_blocks(slot_of, lengths, tokens, weights, dp, ctx):
    devices, piece, width = tokens.shape
    rows = devices * piece
    depth = weights.shape[0]
    groups = devices // 4
    chunk = rows // groups
    seq = 4 * rows
    dma = pltpu.SemaphoreType.DMA
    return pl.pallas_call(
        functools.partial(whole_kernel, dp, ctx, chunk),
        out_shape=jax.ShapeDtypeStruct((rows, HEADS * HEAD_DIM), jnp.bfloat16),
        in_specs=[
            pl.BlockSpec(memory_space=pltpu.SMEM),
            pl.BlockSpec(memory_space=pltpu.SMEM),
            pl.BlockSpec(memory_space=pl.ANY),
            pl.BlockSpec(memory_space=pl.ANY),
        ],
        out_specs=pl.BlockSpec(memory_space=pl.ANY),
        scratch_shapes=[
            pltpu.VMEM((devices, piece, width), jnp.bfloat16),
            pltpu.VMEM((rows, width), jnp.bfloat16),
            pltpu.VMEM((2, lengths.shape[1], HEAD_DIM), jnp.int32),
            pltpu.VMEM((seq, width), jnp.bfloat16),
            pltpu.VMEM((dp, depth, PART_W), jnp.bfloat16),
            pltpu.VMEM((seq // 2, PART_W), jnp.float32),
            pltpu.VMEM((seq, HEAD_DIM), jnp.bfloat16),
            pltpu.VMEM((seq, HEAD_DIM), jnp.bfloat16),
            pltpu.VMEM((seq // 2, Q_W), jnp.bfloat16),
            pltpu.VMEM((seq // 2, Q_W), jnp.float32),
            pltpu.VMEM((2, rows * 2, Q_W), jnp.bfloat16),
            pltpu.VMEM((3, seq, HEAD_DIM), jnp.float32),
            dma, dma((2,)), dma((4,)), dma, dma,
            dma((2, groups)), dma((2, groups)),
            dma((2, groups)), dma((2, groups)),
            dma((2, 2, groups)), dma((2, 2, groups)),
            dma((5, 4)), dma((5, 4)),
            dma((2, 2, 4)), dma((2, 2, 4)),
            dma((2,)), dma((2, devices)), dma((2, devices)),
        ],
        compiler_params=pltpu.CompilerParams(
            collective_id=0, has_side_effects=True, vmem_limit_bytes=48 * 2**20
        ),
    )(slot_of, lengths, tokens, weights)


def on_device(dp, ctx, tokens, projection, placement, doc_lengths):
    row_count, width = tokens.shape
    dev_count = placement.shape[1]
    piece_rows = row_count // dev_count
    destinations = placement[0]
    index = jnp.arange(dev_count, dtype=jnp.int32)
    slot_of = jnp.sum(jnp.where(destinations[None, :] == index[:, None], index[None, :], 0), axis=1)
    pieces = tokens.reshape(dev_count, piece_rows, width)
    if dp == 8 and ctx == 4 and piece_rows == 8:
        blocks = attended_blocks(slot_of, doc_lengths, pieces, projection, dp, ctx)
    else:
        c = lax.axis_index("ctx")
        arrived = lax.all_to_all(pieces[slot_of], ("dp", "ctx"), split_axis=0, concat_axis=0, tiled=True)
        rows = lax.all_gather(arrived.reshape(row_count, width), "ctx", axis=0, tiled=True)
        cuts = [
            lax.dynamic_slice_in_dim(projection, base + c * w, w, axis=1)
            for base, w in ((0, Q_W), (HEADS * HEAD_DIM, HEAD_DIM), ((HEADS + KV_HEADS) * HEAD_DIM, HEAD_DIM))
        ]
        weights = lax.all_gather(jnp.concatenate(cuts, axis=1), "dp", axis=0, tiled=True)
        projected = jnp.dot(rows, weights, preferred_element_type=jnp.float32).astype(jnp.bfloat16)
        mixed = attention(projected, doc_lengths[0])
        by_source = jnp.transpose(mixed.reshape(ctx, dev_count, piece_rows, Q_W), (1, 0, 2, 3))
        returned = lax.all_to_all(by_source, ("dp", "ctx"), split_axis=0, concat_axis=0, tiled=True)
        parts = returned.reshape(dp, ctx, ctx, piece_rows, Q_W)
        blocks = jnp.transpose(parts, (0, 2, 3, 1, 4))
    blocks = blocks.reshape(dev_count, piece_rows, HEADS * HEAD_DIM)
    return blocks[destinations].reshape(row_count, HEADS * HEAD_DIM)


def solution(mesh):
    return jax.shard_map(
        functools.partial(on_device, mesh.shape["dp"], mesh.shape["ctx"]),
        mesh=mesh,
        in_specs=(P(("dp", "ctx"), None), P("dp", None), P(("dp", "ctx"), None), P("dp", None)),
        out_specs=P(("dp", "ctx"), None),
        check_vma=False,
    )
```

```python
import functools
import math

import jax
import jax.numpy as jnp
from jax import lax
from jax.experimental import pallas as pl
from jax.experimental.pallas import tpu as pltpu
from jax.sharding import PartitionSpec as P

HEAD_DIM = 128
HEADS = 16
KV_HEADS = 4
GROUP = HEADS // KV_HEADS
Q_W = GROUP * HEAD_DIM
PART_W = Q_W + 2 * HEAD_DIM
MOST = 512
MESH = pl.DeviceIdType.MESH

theta_base = 500000.0


def position_tables(lengths, seq):
    position = jnp.arange(seq, dtype=jnp.int32)
    ends = jnp.cumsum(lengths)
    begins = jnp.max(
        jnp.where(position[:, None] >= ends[None, :], ends[None, :], 0), axis=1
    )
    half = HEAD_DIM // 2
    frequency = theta_base ** (-2.0 * jnp.arange(half, dtype=jnp.float32) / HEAD_DIM)
    angles = (position - begins).astype(jnp.float32)[:, None] * frequency[None, :]
    cosine, sine = jnp.cos(angles), jnp.sin(angles)
    return (
        jnp.concatenate([cosine, cosine], axis=1),
        jnp.concatenate([-sine, sine], axis=1),
        jnp.broadcast_to(begins[:, None].astype(jnp.float32), (seq, HEAD_DIM)),
    )


def attention_kernel(block, proj_ref, cos_ref, sin_ref, begin_ref, out_ref, key_ref):
    seq = proj_ref.shape[0]
    factor = HEAD_DIM**-0.5 * math.log2(math.e)

    def rotated(rows, column):
        x = proj_ref[rows, column : column + HEAD_DIM].astype(jnp.float32)
        turned = pltpu.roll(x, HEAD_DIM // 2, 1)
        return (x * cos_ref[rows, :] + turned * sin_ref[rows, :]).astype(jnp.bfloat16)

    for b in range(seq // block):
        rows = slice(b * block, (b + 1) * block)
        key_ref[rows, :] = rotated(rows, Q_W)
    for b in range(seq // block):
        rows = slice(b * block, (b + 1) * block)
        first = max(0, (b * block - (MOST - 1)) // block * block)
        keys = slice(first, (b + 1) * block)
        width = (b + 1) * block - first
        at = first + lax.broadcasted_iota(jnp.int32, (block, width), 1)
        own = b * block + lax.broadcasted_iota(jnp.int32, (block, width), 0)
        allowed = (at.astype(jnp.float32) >= begin_ref[rows, 0:1]) & (at <= own)
        values = proj_ref[keys, Q_W + HEAD_DIM : PART_W]
        for h in range(GROUP):
            scores = lax.dot_general(
                rotated(rows, h * HEAD_DIM),
                key_ref[keys, :],
                (((1,), (1,)), ((), ())),
                preferred_element_type=jnp.float32,
            )
            scores = jnp.where(allowed, scores, -jnp.inf)
            top = jnp.max(scores, axis=1, keepdims=True)
            weights = jnp.exp2((scores - top) * factor)
            total = jnp.sum(weights, axis=1, keepdims=True)
            mixed = jnp.dot(
                weights.astype(jnp.bfloat16), values, preferred_element_type=jnp.float32
            )
            out_ref[rows, h * HEAD_DIM : (h + 1) * HEAD_DIM] = (mixed / total).astype(jnp.bfloat16)


def attention(projected, lengths):
    seq = projected.shape[0]
    cosine, sine, begins = position_tables(lengths, seq)
    return pl.pallas_call(
        functools.partial(attention_kernel, 256),
        out_shape=jax.ShapeDtypeStruct((seq, Q_W), jnp.bfloat16),
        in_specs=[pl.BlockSpec(memory_space=pltpu.VMEM)] * 4,
        out_specs=pl.BlockSpec(memory_space=pltpu.VMEM),
        scratch_shapes=[pltpu.VMEM((seq, HEAD_DIM), jnp.bfloat16)],
        compiler_params=pltpu.CompilerParams(vmem_limit_bytes=32 * 2**20),
    )(projected, cosine, sine, begins)


PHASES = (
    ((HEADS * HEAD_DIM, HEAD_DIM, 0, HEAD_DIM), ((HEADS + KV_HEADS) * HEAD_DIM, HEAD_DIM, HEAD_DIM, HEAD_DIM),
     (0, Q_W, 2 * HEAD_DIM, Q_W // 2)),
    ((Q_W // 2, Q_W, 2 * HEAD_DIM + Q_W // 2, Q_W // 2),),
)

PHASE_COLUMNS = ((0, 2 * HEAD_DIM + Q_W // 2), (2 * HEAD_DIM + Q_W // 2, Q_W // 2))
PHASE_HEADS = (range(0, GROUP // 2), range(GROUP // 2, GROUP))
RET_W = Q_W // 2


def whole_kernel(dp, ctx, chunk, slot_ref, len_ref, tok_hbm, w_ref, ret_ref,
                 tok_ref, stage, ends, x_ref, w_buf, acc_ref, key_ref, val_ref, qry_ref, mix_ref, out_buf, tabs,
                 in_sem, own_sem, wown_sem, tab_send, tab_recv, tok_send, tok_recv, z_send, z_recv,
                 c_send, c_recv, w_send, w_recv, f_send, f_recv, r_own, r_send, r_recv):
    d, c = lax.axis_index("dp"), lax.axis_index("ctx")
    devices = dp * ctx
    me = d * ctx + c
    dc, cz = d % 2, c % 2
    groups = devices // 4
    halves = ctx // 2
    s_me = (d // 2) * halves + c // 2
    m_me = dc * 2 + cz
    m_z = dc * 2 + 1 - cz
    d_sib, c_sib = d + 1 - 2 * dc, c + 1 - 2 * cz
    part = chunk // 2
    slab = groups * part
    depth = w_ref.shape[0]
    piece = chunk // ctx
    block = devices * piece
    seq = ctx * block
    rows_half = seq // 2
    quarters = ctx // 2

    def class_peer(s):
        return ((s // halves) * 2 + dc, (s % halves) * 2 + cz)

    def remote(src, dst, send, recv, device):
        return pltpu.make_async_remote_copy(
            src_ref=src, dst_ref=dst, send_sem=send, recv_sem=recv, device_id=device, device_id_type=MESH
        )

    tok_in = pltpu.make_async_copy(tok_hbm, tok_ref, in_sem)
    tok_in.start()

    barrier = pltpu.get_barrier_semaphore()

    @pl.loop(1, devices)
    def _(t):
        other = (me + t) % devices
        pl.semaphore_signal(barrier, inc=1, device_id=(other // ctx, other % ctx), device_id_type=MESH)

    document = lax.broadcasted_iota(jnp.int32, ends.shape[1:], 0)
    end, table = jnp.int32(0), jnp.zeros(ends.shape[1:], jnp.int32)
    for j in range(ends.shape[1]):
        end = end + len_ref[0, j]
        table = jnp.where(document == j, end, table)
    ends[dc] = table

    pl.semaphore_wait(barrier, devices - 1)

    def gather(s, h):
        at = s * ctx + h * quarters
        rows = [tok_ref[slot_ref[at + q]] for q in range(quarters)]
        start = pl.multiple_of(s * chunk + h * part, part)
        stage[pl.ds(start, part), :] = jnp.concatenate(rows, axis=0)

    def x_rows(m, s, h):
        return x_ref.at[pl.ds(pl.multiple_of(h * rows_half + m * slab + s * part, part), part), :]

    def tok_rows(s, h):
        return stage.at[pl.ds(pl.multiple_of(s * chunk + h * part, part), part), :]

    def own_copy(h):
        return pltpu.make_async_copy(tok_rows(s_me, h), x_rows(m_me, s_me, h), own_sem.at[h])

    def tok_copy(t, h):
        s = (s_me + t) % groups
        return remote(tok_rows(s, h), x_rows(m_me, s_me, h), tok_send.at[h, t], tok_recv.at[h, t], class_peer(s))

    tab_out = remote(ends.at[dc], ends.at[dc], tab_send, tab_recv, (d_sib, c))
    tab_in = remote(ends.at[1 - dc], ends.at[1 - dc], tab_send, tab_recv, (d_sib, c))

    chip = d // 2
    chip_x = chip + 1 - 2 * (chip % 2)
    chip_y = (chip + 2) % 4
    chip_far = (chip_x + 2) % 4

    def w_parts(d_to, d_from, phase):
        g = (d_to % 2) * 2 + cz
        for i, (base, stride, to, width) in enumerate(PHASES[phase]):
            start = pl.multiple_of(base + g * stride, HEAD_DIM)
            yield (w_ref.at[:, pl.ds(start, width)], w_buf.at[d_from, :, to : to + width], 3 * phase + i)

    near = ((0, d_sib), (1, chip_x * 2 + dc), (2, chip_x * 2 + 1 - dc), (3, chip_y * 2 + dc), (4, chip_y * 2 + 1 - dc))

    def w_out(phase, slots=range(5)):
        return [remote(src, dst, w_send.at[slot, i], w_recv.at[slot, i], (d_to, c))
                for slot, d_to in near if slot in slots for src, dst, i in w_parts(d_to, d, phase)]

    def w_in(phase, slots):
        return [remote(src, dst, w_send.at[slot, i], w_recv.at[slot, i], (d_from, c))
                for slot, d_from in near if slot in slots for src, dst, i in w_parts(d, d_from, phase)]

    w_own = [pltpu.make_async_copy(src, dst, wown_sem.at[i])
             for phase in range(2) for src, dst, i in w_parts(d, d, phase)]

    half = depth // 2

    def f_parts(chip_from, way, phase, chip_to):
        for core in range(2):
            for i, (_, _, to, width) in enumerate(PHASES[phase]):
                there = w_buf.at[chip_from * 2 + core, way * half : (way + 1) * half, to : to + width]
                yield remote(there, there, f_send.at[way, core, 3 * phase + i], f_recv.at[way, core, 3 * phase + i],
                             (chip_to * 2 + dc, c))

    def f_out(phase, way):
        return list(f_parts((chip_x, chip_y)[way], way, phase, (chip_y, chip_x)[way]))

    def f_in(phase, way):
        return list(f_parts(chip_far, way, phase, (chip_y, chip_x)[way]))

    def came(t):
        return (s_me - t + groups) % groups

    def tok_arrival(t, h):
        return remote(tok_rows(came(t), h), x_rows(m_me, came(t), h), tok_send.at[h, t], tok_recv.at[h, t],
                      class_peer(came(t)))

    def z_copy(t, h):
        to = x_rows(m_me, came(t), h)
        at = to if t else tok_rows(s_me, h)
        return remote(at, to, z_send.at[h, t], z_recv.at[h, t], (d, c_sib))

    def z_arrival(t, h):
        at = x_rows(m_z, came(t), h)
        return remote(at, at, z_send.at[h, t], z_recv.at[h, t], (d, c_sib))

    def c_copy(which, t, h):
        to = x_rows(m_z if which else m_me, came(t), h)
        at = to if t or which else tok_rows(s_me, h)
        return remote(at, to, c_send.at[h, which, t], c_recv.at[h, which, t], (d_sib, c))

    def c_arrival(which, t, h):
        at = x_rows((1 - dc) * 2 + (1 - cz if which else cz), came(t), h)
        return remote(at, at, c_send.at[h, which, t], c_recv.at[h, which, t], (d_sib, c))

    def forward_class(h, ts):
        for t in ts:
            tok_arrival(t, h).wait_recv()
            z_copy(t, h).start()
            c_copy(0, t, h).start()

    def forward_z(h, ts):
        for t in ts:
            z_arrival(t, h).wait_recv()
            c_copy(1, t, h).start()

    def start_own(h):
        gather(s_me, h)
        z_copy(0, h).start()
        c_copy(0, 0, h).start()
        own_copy(h).start()

    tab_out.start()
    tok_in.wait()
    for t in range(1, groups):
        gather((s_me + t) % groups, 0)
        tok_copy(t, 0).start()
        if t == 1:
            start_own(0)
        for copy in w_out(0, (t,) if t < 5 else ()):
            copy.start()
    for copy in w_out(0, (0,)):
        copy.start()
    for copy in w_own:
        copy.start()

    for t in range(1, groups):
        gather((s_me + t) % groups, 1)
    start_own(1)
    forward_class(0, range(1, groups))
    for t in range(1, groups):
        tok_copy(t, 1).start()

    tab_in.wait_recv()

    @pl.loop(0, seq // 64)
    def _(n):
        rows = pl.ds(pl.multiple_of(n * 64, 64), 64)
        position = n * 64 + lax.broadcasted_iota(jnp.int32, (64, HEAD_DIM), 0)
        lane = lax.broadcasted_iota(jnp.int32, (1, HEAD_DIM), 1)
        begin = jnp.zeros((64, HEAD_DIM), jnp.int32)
        for j in range(ends.shape[1]):
            end = ends[c // 2, j : j + 1, :]
            begin = jnp.maximum(begin, jnp.where(position >= end, end, 0))
        spread = (lane % (HEAD_DIM // 2)).astype(jnp.float32) * (-2.0 * math.log(theta_base) / HEAD_DIM)
        angles = (position - begin).astype(jnp.float32) * jnp.exp(spread)
        sine = jnp.sin(angles)
        tabs[0, rows, :] = jnp.cos(angles)
        tabs[1, rows, :] = jnp.where(lane < HEAD_DIM // 2, -sine, sine)
        tabs[2, rows, :] = begin.astype(jnp.float32)

    def forward_weights(phase):
        for way in range(2):
            for copy in w_in(phase, ((1, 2), (3, 4))[way]):
                copy.wait_recv()
            for copy in f_out(phase, way):
                copy.start()

    forward_z(0, range(groups // 2))
    forward_weights(0)
    for copy in w_out(1):
        copy.start()
    forward_z(0, range(groups // 2, groups))
    forward_class(1, range(1, groups))

    def rows_of(i, q, first):
        src_d, src_c = i // ctx, i % ctx
        m = (src_d % 2) * 2 + src_c % 2
        s = (src_d // 2) * halves + src_c // 2
        start = pl.multiple_of(m * slab + s * part + q * piece, piece)
        return acc_ref[pl.ds(start, piece), first : first + HEAD_DIM]

    def rotate(x, at):
        x = x.astype(jnp.bfloat16).astype(jnp.float32)
        turned = pltpu.roll(x, HEAD_DIM // 2, 1)
        cosine = tabs[0, pl.ds(at, 2 * piece), :]
        sine = tabs[1, pl.ds(at, 2 * piece), :]
        return (x * cosine + turned * sine).astype(jnp.bfloat16)

    def pack(half_at, phase):
        @pl.loop(0, devices // 2, unroll=4)
        def _(pair):
            for q in range(quarters):
                def both(first):
                    return jnp.concatenate([rows_of(pair * 2 + i, q, first) for i in range(2)], axis=0)

                near_at = pl.multiple_of(q * block + pair * 2 * piece, 2 * piece)
                at = pl.multiple_of(half_at * rows_half + near_at, 2 * piece)
                to = pl.ds(at, 2 * piece)
                if phase == 0:
                    key_ref[to, :] = rotate(both(0), at)
                    val_ref[to, :] = both(HEAD_DIM).astype(jnp.bfloat16)
                for h in PHASE_HEADS[phase]:
                    qry_ref[pl.ds(near_at, 2 * piece), h * HEAD_DIM : (h + 1) * HEAD_DIM] = rotate(
                        both((2 + h) * HEAD_DIM), at)

    factor = HEAD_DIM**-0.5 * math.log2(math.e)

    def attend(half_at, phase):
        for j in range(quarters):
            b = half_at * quarters + j
            rows = slice(b * block, (b + 1) * block)
            near_rows = slice(j * block, (j + 1) * block)
            first = max(0, (b * block - (MOST - 1)) // block * block)
            keys = slice(first, (b + 1) * block)
            width = (b + 1) * block - first
            at = first + lax.broadcasted_iota(jnp.int32, (block, width), 1)
            at_own = b * block + lax.broadcasted_iota(jnp.int32, (block, width), 0)
            begin = tabs[2, rows, 0:1]
            allowed = (at.astype(jnp.float32) >= begin) & (at <= at_own)
            for h in PHASE_HEADS[phase]:
                scores = lax.dot_general(
                    qry_ref[near_rows, h * HEAD_DIM : (h + 1) * HEAD_DIM], key_ref[keys, :],
                    (((1,), (1,)), ((), ())), preferred_element_type=jnp.float32,
                )
                scores = jnp.where(allowed, scores, -jnp.inf)
                top = jnp.max(scores, axis=1, keepdims=True)
                weights = jnp.exp2((scores - top) * factor)
                total = jnp.sum(weights, axis=1, keepdims=True)
                mixed = jnp.dot(weights.astype(jnp.bfloat16), val_ref[keys, :],
                                preferred_element_type=jnp.float32)
                mix_ref[near_rows, h * HEAD_DIM : (h + 1) * HEAD_DIM] = mixed / total

    def ret_at(s, m, h, phase):
        return ret_ref.at[pl.ds(pl.multiple_of(s * chunk + h * part, part), part),
                          pl.ds(pl.multiple_of(m * Q_W + phase * RET_W, RET_W), RET_W)]

    def buf_at(i, h, phase):
        return out_buf.at[h, phase, pl.ds(pl.multiple_of(i * part, part), part), :]

    def ret_copy(h, phase, t):
        i = (me + t) % devices
        return remote(buf_at(i, h, phase), ret_at(s_me, m_me, h, phase), r_send.at[h, phase, t],
                      r_recv.at[h, phase, t], (i // ctx, i % ctx))

    def ret_arrival(h, phase, t):
        i = (me - t + devices) % devices
        src_d, src_c = i // ctx, i % ctx
        s = (src_d // 2) * halves + src_c // 2
        m = (src_d % 2) * 2 + src_c % 2
        return remote(buf_at(i, h, phase), ret_at(s, m, h, phase), r_send.at[h, phase, t],
                      r_recv.at[h, phase, t], (src_d, src_c))

    def own_ret(h, phase):
        return pltpu.make_async_copy(buf_at(me, h, phase), ret_at(s_me, m_me, h, phase), r_own.at[h, phase])

    def send_back(h, phase):
        def ready(i):
            parts = [
                mix_ref[pl.ds(pl.multiple_of(q * block + i * piece, piece), piece),
                        phase * RET_W : (phase + 1) * RET_W]
                for q in range(quarters)
            ]
            out_buf[h, phase, pl.ds(pl.multiple_of(i * part, part), part), :] = (
                jnp.concatenate(parts, axis=0).astype(jnp.bfloat16))

        @pl.loop(1, devices)
        def _(t):
            ready((me + t) % devices)
            ret_copy(h, phase, t).start()

        ready(me)
        own_ret(h, phase).start()

    def finish(h, phase):
        pack(h, phase)
        attend(h, phase)
        send_back(h, phase)

    own_copy(0).wait()
    for t in range(groups):
        for which in range(2):
            c_arrival(which, t, 0).wait_recv()
    for copy in w_own:
        copy.wait()

    def multiply(rows, k, start, extent, phase):
        columns = pl.ds(pl.multiple_of(k * depth + start, extent), extent)
        first, width = PHASE_COLUMNS[phase]
        return jnp.dot(x_ref[rows, columns], w_buf[k, start : start + extent, first : first + width],
                       preferred_element_type=jnp.float32)

    def place(phase):
        first, width = PHASE_COLUMNS[phase]
        return slice(first, first + width)

    def whole(to, rows, phase):
        acc_ref[to, place(phase)] = multiply(rows, 0, 0, depth, phase)

        @pl.loop(1, dp)
        def _(k):
            acc_ref[to, place(phase)] += multiply(rows, k, 0, depth, phase)

    early = pl.ds(0, rows_half)
    acc_ref[:, place(0)] = multiply(early, d, 0, depth, 0)
    for copy in w_in(0, (0,)):
        copy.wait_recv()
    for _, d_from in near:
        acc_ref[:, place(0)] += multiply(early, d_from, 0, depth, 0)
    forward_z(1, range(groups // 4))
    for way in range(2):
        for copy in f_in(0, way):
            copy.wait_recv()
        for core in range(2):
            acc_ref[:, place(0)] += multiply(early, chip_far * 2 + core, way * half, half, 0)
    forward_z(1, range(groups // 4, groups // 2))
    forward_weights(1)
    finish(0, 0)

    forward_z(1, range(groups // 2, groups))
    own_copy(1).wait()
    for which in range(2):
        if which:
            for t in range(groups):
                c_arrival(0, t, 1).wait_recv()
                c_arrival(1, t, 1).wait_recv()
        base = (1 - dc if which else dc) * 2 * slab
        whole(pl.ds(pl.multiple_of(base, 2 * slab), 2 * slab),
              pl.ds(pl.multiple_of(rows_half + base, 2 * slab), 2 * slab), 0)
    finish(1, 0)

    for copy in w_in(1, (0,)) + f_in(1, 0) + f_in(1, 1):
        copy.wait_recv()
    for h in range(2):
        whole(early, pl.ds(h * rows_half, rows_half), 1)
        finish(h, 1)

    tab_out.wait_send()
    for copy in w_out(0) + w_out(1) + [copy for way in range(2) for phase in range(2) for copy in f_out(phase, way)]:
        copy.wait_send()
    for h in range(2):
        for t in range(groups):
            if t > 0:
                tok_copy(t, h).wait_send()
            z_copy(t, h).wait_send()
            c_copy(0, t, h).wait_send()
            c_copy(1, t, h).wait_send()
        for phase in range(2):
            own_ret(h, phase).wait()

            @pl.loop(1, devices)
            def _(t):
                ret_copy(h, phase, t).wait_send()
                ret_arrival(h, phase, t).wait_recv()


def attended_blocks(slot_of, lengths, tokens, weights, dp, ctx):
    devices, piece, width = tokens.shape
    rows = devices * piece
    depth = weights.shape[0]
    groups = devices // 4
    chunk = rows // groups
    seq = 4 * rows
    dma = pltpu.SemaphoreType.DMA
    return pl.pallas_call(
        functools.partial(whole_kernel, dp, ctx, chunk),
        out_shape=jax.ShapeDtypeStruct((rows, HEADS * HEAD_DIM), jnp.bfloat16),
        in_specs=[
            pl.BlockSpec(memory_space=pltpu.SMEM),
            pl.BlockSpec(memory_space=pltpu.SMEM),
            pl.BlockSpec(memory_space=pltpu.HBM),
            pl.BlockSpec(memory_space=pltpu.HBM),
        ],
        out_specs=pl.BlockSpec(memory_space=pl.ANY),
        scratch_shapes=[
            pltpu.VMEM((devices, piece, width), jnp.bfloat16),
            pltpu.VMEM((rows, width), jnp.bfloat16),
            pltpu.VMEM((2, lengths.shape[1], HEAD_DIM), jnp.int32),
            pltpu.VMEM((seq, width), jnp.bfloat16),
            pltpu.VMEM((dp, depth, PART_W), jnp.bfloat16),
            pltpu.VMEM((seq // 2, PART_W), jnp.float32),
            pltpu.VMEM((seq, HEAD_DIM), jnp.bfloat16),
            pltpu.VMEM((seq, HEAD_DIM), jnp.bfloat16),
            pltpu.VMEM((seq // 2, Q_W), jnp.bfloat16),
            pltpu.VMEM((seq // 2, Q_W), jnp.float32),
            pltpu.VMEM((2, 2, rows * 2, RET_W), jnp.bfloat16),
            pltpu.VMEM((3, seq, HEAD_DIM), jnp.float32),
            dma, dma((2,)), dma((4,)), dma, dma,
            dma((2, groups)), dma((2, groups)),
            dma((2, groups)), dma((2, groups)),
            dma((2, 2, groups)), dma((2, 2, groups)),
            dma((5, 4)), dma((5, 4)),
            dma((2, 2, 4)), dma((2, 2, 4)),
            dma((2, 2)), dma((2, 2, devices)), dma((2, 2, devices)),
        ],
        compiler_params=pltpu.CompilerParams(
            collective_id=0, has_side_effects=True, vmem_limit_bytes=48 * 2**20
        ),
    )(slot_of, lengths, tokens, weights)


def on_device(dp, ctx, tokens, projection, placement, doc_lengths):
    row_count, width = tokens.shape
    dev_count = placement.shape[1]
    piece_rows = row_count // dev_count
    destinations = placement[0]
    index = jnp.arange(dev_count, dtype=jnp.int32)
    slot_of = jnp.sum(jnp.where(destinations[None, :] == index[:, None], index[None, :], 0), axis=1)
    pieces = tokens.reshape(dev_count, piece_rows, width)
    if dp == 8 and ctx == 4 and piece_rows == 8:
        blocks = attended_blocks(slot_of, doc_lengths, pieces, projection, dp, ctx)
    else:
        c = lax.axis_index("ctx")
        arrived = lax.all_to_all(pieces[slot_of], ("dp", "ctx"), split_axis=0, concat_axis=0, tiled=True)
        rows = lax.all_gather(arrived.reshape(row_count, width), "ctx", axis=0, tiled=True)
        cuts = [
            lax.dynamic_slice_in_dim(projection, base + c * w, w, axis=1)
            for base, w in ((0, Q_W), (HEADS * HEAD_DIM, HEAD_DIM), ((HEADS + KV_HEADS) * HEAD_DIM, HEAD_DIM))
        ]
        weights = lax.all_gather(jnp.concatenate(cuts, axis=1), "dp", axis=0, tiled=True)
        projected = jnp.dot(rows, weights, preferred_element_type=jnp.float32).astype(jnp.bfloat16)
        mixed = attention(projected, doc_lengths[0])
        by_source = jnp.transpose(mixed.reshape(ctx, dev_count, piece_rows, Q_W), (1, 0, 2, 3))
        returned = lax.all_to_all(by_source, ("dp", "ctx"), split_axis=0, concat_axis=0, tiled=True)
        parts = returned.reshape(dp, ctx, ctx, piece_rows, Q_W)
        blocks = jnp.transpose(parts, (0, 2, 3, 1, 4))
    blocks = blocks.reshape(dev_count, piece_rows, HEADS * HEAD_DIM)
    return blocks[destinations].reshape(row_count, HEADS * HEAD_DIM)


def solution(mesh):
    return jax.shard_map(
        functools.partial(on_device, mesh.shape["dp"], mesh.shape["ctx"]),
        mesh=mesh,
        in_specs=(P(("dp", "ctx"), None), P("dp", None), P(("dp", "ctx"), None), P("dp", None)),
        out_specs=P(("dp", "ctx"), None),
        check_vma=False,
    )
```

```python
import functools
import math

import jax
import jax.numpy as jnp
from jax import lax
from jax.experimental import pallas as pl
from jax.experimental.pallas import tpu as pltpu
from jax.sharding import PartitionSpec as P

HEAD_DIM = 128
HEADS = 16
KV_HEADS = 4
GROUP = HEADS // KV_HEADS
Q_W = GROUP * HEAD_DIM
PART_W = Q_W + 2 * HEAD_DIM
MOST = 512
MESH = pl.DeviceIdType.MESH

theta_base = 500000.0


def position_tables(lengths, seq):
    position = jnp.arange(seq, dtype=jnp.int32)
    ends = jnp.cumsum(lengths)
    begins = jnp.max(
        jnp.where(position[:, None] >= ends[None, :], ends[None, :], 0), axis=1
    )
    half = HEAD_DIM // 2
    frequency = theta_base ** (-2.0 * jnp.arange(half, dtype=jnp.float32) / HEAD_DIM)
    angles = (position - begins).astype(jnp.float32)[:, None] * frequency[None, :]
    cosine, sine = jnp.cos(angles), jnp.sin(angles)
    return (
        jnp.concatenate([cosine, cosine], axis=1),
        jnp.concatenate([-sine, sine], axis=1),
        jnp.broadcast_to(begins[:, None].astype(jnp.float32), (seq, HEAD_DIM)),
    )


def attention_kernel(block, proj_ref, cos_ref, sin_ref, begin_ref, out_ref, key_ref):
    seq = proj_ref.shape[0]
    factor = HEAD_DIM**-0.5 * math.log2(math.e)

    def rotated(rows, column):
        x = proj_ref[rows, column : column + HEAD_DIM].astype(jnp.float32)
        turned = pltpu.roll(x, HEAD_DIM // 2, 1)
        return (x * cos_ref[rows, :] + turned * sin_ref[rows, :]).astype(jnp.bfloat16)

    for b in range(seq // block):
        rows = slice(b * block, (b + 1) * block)
        key_ref[rows, :] = rotated(rows, Q_W)
    for b in range(seq // block):
        rows = slice(b * block, (b + 1) * block)
        first = max(0, (b * block - (MOST - 1)) // block * block)
        keys = slice(first, (b + 1) * block)
        width = (b + 1) * block - first
        at = first + lax.broadcasted_iota(jnp.int32, (block, width), 1)
        own = b * block + lax.broadcasted_iota(jnp.int32, (block, width), 0)
        allowed = (at.astype(jnp.float32) >= begin_ref[rows, 0:1]) & (at <= own)
        values = proj_ref[keys, Q_W + HEAD_DIM : PART_W]
        for h in range(GROUP):
            scores = lax.dot_general(
                rotated(rows, h * HEAD_DIM),
                key_ref[keys, :],
                (((1,), (1,)), ((), ())),
                preferred_element_type=jnp.float32,
            )
            scores = jnp.where(allowed, scores, -jnp.inf)
            top = jnp.max(scores, axis=1, keepdims=True)
            weights = jnp.exp2((scores - top) * factor)
            total = jnp.sum(weights, axis=1, keepdims=True)
            mixed = jnp.dot(
                weights.astype(jnp.bfloat16), values, preferred_element_type=jnp.float32
            )
            out_ref[rows, h * HEAD_DIM : (h + 1) * HEAD_DIM] = (mixed / total).astype(jnp.bfloat16)


def attention(projected, lengths):
    seq = projected.shape[0]
    cosine, sine, begins = position_tables(lengths, seq)
    return pl.pallas_call(
        functools.partial(attention_kernel, 256),
        out_shape=jax.ShapeDtypeStruct((seq, Q_W), jnp.bfloat16),
        in_specs=[pl.BlockSpec(memory_space=pltpu.VMEM)] * 4,
        out_specs=pl.BlockSpec(memory_space=pltpu.VMEM),
        scratch_shapes=[pltpu.VMEM((seq, HEAD_DIM), jnp.bfloat16)],
        compiler_params=pltpu.CompilerParams(vmem_limit_bytes=32 * 2**20),
    )(projected, cosine, sine, begins)


PHASES = (
    ((HEADS * HEAD_DIM, HEAD_DIM, 0, HEAD_DIM), ((HEADS + KV_HEADS) * HEAD_DIM, HEAD_DIM, HEAD_DIM, HEAD_DIM),
     (0, Q_W, 2 * HEAD_DIM, Q_W // 2)),
    ((Q_W // 2, Q_W, 2 * HEAD_DIM + Q_W // 2, Q_W // 2),),
)

PHASE_COLUMNS = ((0, 2 * HEAD_DIM + Q_W // 2), (2 * HEAD_DIM + Q_W // 2, Q_W // 2))
PHASE_HEADS = (range(0, GROUP // 2), range(GROUP // 2, GROUP))
RET_W = Q_W // 2


def whole_kernel(dp, ctx, chunk, slot_ref, len_ref, tok_hbm, w_ref, ret_ref,
                 tok_ref, stage, ends, x_ref, w_buf, acc_ref, key_ref, val_ref, qry_ref, mix_ref, out_buf, tabs,
                 in_sem, own_sem, wown_sem, tab_send, tab_recv, tok_send, tok_recv, z_send, z_recv,
                 c_send, c_recv, w_send, w_recv, f_send, f_recv, r_own, r_send, r_recv):
    d, c = lax.axis_index("dp"), lax.axis_index("ctx")
    devices = dp * ctx
    me = d * ctx + c
    dc, cz = d % 2, c % 2
    groups = devices // 4
    halves = ctx // 2
    s_me = (d // 2) * halves + c // 2
    m_me = dc * 2 + cz
    m_z = dc * 2 + 1 - cz
    d_sib, c_sib = d + 1 - 2 * dc, c + 1 - 2 * cz
    part = chunk // 2
    slab = groups * part
    depth = w_ref.shape[0]
    piece = chunk // ctx
    block = devices * piece
    seq = ctx * block
    rows_half = seq // 2
    quarters = ctx // 2

    def class_peer(s):
        return ((s // halves) * 2 + dc, (s % halves) * 2 + cz)

    def remote(src, dst, send, recv, device):
        return pltpu.make_async_remote_copy(
            src_ref=src, dst_ref=dst, send_sem=send, recv_sem=recv, device_id=device, device_id_type=MESH
        )

    tok_in = pltpu.make_async_copy(tok_hbm, tok_ref, in_sem)
    tok_in.start()

    barrier = pltpu.get_barrier_semaphore()

    @pl.loop(1, devices)
    def _(t):
        other = (me + t) % devices
        pl.semaphore_signal(barrier, inc=1, device_id=(other // ctx, other % ctx), device_id_type=MESH)

    document = lax.broadcasted_iota(jnp.int32, ends.shape[1:], 0)
    end, table = jnp.int32(0), jnp.zeros(ends.shape[1:], jnp.int32)
    for j in range(ends.shape[1]):
        end = end + len_ref[0, j]
        table = jnp.where(document == j, end, table)
    ends[dc] = table

    pl.semaphore_wait(barrier, devices - 1)

    def gather(s, h):
        at = s * ctx + h * quarters
        rows = [tok_ref[slot_ref[at + q]] for q in range(quarters)]
        start = pl.multiple_of(s * chunk + h * part, part)
        stage[pl.ds(start, part), :] = jnp.concatenate(rows, axis=0)

    def x_rows(m, s, h):
        return x_ref.at[pl.ds(pl.multiple_of(h * rows_half + m * slab + s * part, part), part), :]

    def tok_rows(s, h):
        return stage.at[pl.ds(pl.multiple_of(s * chunk + h * part, part), part), :]

    def own_copy(h):
        return pltpu.make_async_copy(tok_rows(s_me, h), x_rows(m_me, s_me, h), own_sem.at[h])

    def tok_copy(t, h):
        s = (s_me + t) % groups
        return remote(tok_rows(s, h), x_rows(m_me, s_me, h), tok_send.at[h, t], tok_recv.at[h, t], class_peer(s))

    tab_out = remote(ends.at[dc], ends.at[dc], tab_send, tab_recv, (d_sib, c))
    tab_in = remote(ends.at[1 - dc], ends.at[1 - dc], tab_send, tab_recv, (d_sib, c))

    chip = d // 2
    chip_x = chip + 1 - 2 * (chip % 2)
    chip_y = (chip + 2) % 4
    chip_far = (chip_x + 2) % 4

    def w_parts(d_to, d_from, phase):
        g = (d_to % 2) * 2 + cz
        for i, (base, stride, to, width) in enumerate(PHASES[phase]):
            start = pl.multiple_of(base + g * stride, HEAD_DIM)
            yield (w_ref.at[:, pl.ds(start, width)], w_buf.at[d_from, :, to : to + width], 3 * phase + i)

    near = ((0, d_sib), (1, chip_x * 2 + dc), (2, chip_x * 2 + 1 - dc), (3, chip_y * 2 + dc), (4, chip_y * 2 + 1 - dc))

    def w_out(phase, slots=range(5)):
        return [remote(src, dst, w_send.at[slot, i], w_recv.at[slot, i], (d_to, c))
                for slot, d_to in near if slot in slots for src, dst, i in w_parts(d_to, d, phase)]

    def w_in(phase, slots):
        return [remote(src, dst, w_send.at[slot, i], w_recv.at[slot, i], (d_from, c))
                for slot, d_from in near if slot in slots for src, dst, i in w_parts(d, d_from, phase)]

    w_own = [pltpu.make_async_copy(src, dst, wown_sem.at[i])
             for phase in range(2) for src, dst, i in w_parts(d, d, phase)]

    half = depth // 2

    def f_parts(chip_from, way, phase, chip_to):
        for core in range(2):
            for i, (_, _, to, width) in enumerate(PHASES[phase]):
                there = w_buf.at[chip_from * 2 + core, way * half : (way + 1) * half, to : to + width]
                yield remote(there, there, f_send.at[way, core, 3 * phase + i], f_recv.at[way, core, 3 * phase + i],
                             (chip_to * 2 + dc, c))

    def f_out(phase, way):
        return list(f_parts((chip_x, chip_y)[way], way, phase, (chip_y, chip_x)[way]))

    def f_in(phase, way):
        return list(f_parts(chip_far, way, phase, (chip_y, chip_x)[way]))

    def came(t):
        return (s_me - t + groups) % groups

    def tok_arrival(t, h):
        return remote(tok_rows(came(t), h), x_rows(m_me, came(t), h), tok_send.at[h, t], tok_recv.at[h, t],
                      class_peer(came(t)))

    def z_copy(t, h):
        to = x_rows(m_me, came(t), h)
        at = to if t else tok_rows(s_me, h)
        return remote(at, to, z_send.at[h, t], z_recv.at[h, t], (d, c_sib))

    def z_arrival(t, h):
        at = x_rows(m_z, came(t), h)
        return remote(at, at, z_send.at[h, t], z_recv.at[h, t], (d, c_sib))

    def c_copy(which, t, h):
        to = x_rows(m_z if which else m_me, came(t), h)
        at = to if t or which else tok_rows(s_me, h)
        return remote(at, to, c_send.at[h, which, t], c_recv.at[h, which, t], (d_sib, c))

    def c_arrival(which, t, h):
        at = x_rows((1 - dc) * 2 + (1 - cz if which else cz), came(t), h)
        return remote(at, at, c_send.at[h, which, t], c_recv.at[h, which, t], (d_sib, c))

    def forward_class(h, ts):
        for t in ts:
            tok_arrival(t, h).wait_recv()
            z_copy(t, h).start()
            c_copy(0, t, h).start()

    def forward_z(h, ts):
        for t in ts:
            z_arrival(t, h).wait_recv()
            c_copy(1, t, h).start()

    def start_own(h):
        gather(s_me, h)
        z_copy(0, h).start()
        c_copy(0, 0, h).start()
        own_copy(h).start()

    tab_out.start()
    tok_in.wait()
    for t in range(1, groups):
        gather((s_me + t) % groups, 0)
        tok_copy(t, 0).start()
        if t == 1:
            start_own(0)
    for t in range(1, groups):
        gather((s_me + t) % groups, 1)
        tok_copy(t, 1).start()
        if t == 1:
            start_own(1)
    forward_class(0, range(1, groups // 2))
    for copy in w_out(0, (1, 3, 2, 4, 0)):
        copy.start()
    for copy in w_own:
        copy.start()

    forward_class(0, range(groups // 2, groups))

    tab_in.wait_recv()

    @pl.loop(0, seq // 64)
    def _(n):
        rows = pl.ds(pl.multiple_of(n * 64, 64), 64)
        position = n * 64 + lax.broadcasted_iota(jnp.int32, (64, HEAD_DIM), 0)
        lane = lax.broadcasted_iota(jnp.int32, (1, HEAD_DIM), 1)
        begin = jnp.zeros((64, HEAD_DIM), jnp.int32)
        for j in range(ends.shape[1]):
            end = ends[c // 2, j : j + 1, :]
            begin = jnp.maximum(begin, jnp.where(position >= end, end, 0))
        spread = (lane % (HEAD_DIM // 2)).astype(jnp.float32) * (-2.0 * math.log(theta_base) / HEAD_DIM)
        angles = (position - begin).astype(jnp.float32) * jnp.exp(spread)
        sine = jnp.sin(angles)
        tabs[0, rows, :] = jnp.cos(angles)
        tabs[1, rows, :] = jnp.where(lane < HEAD_DIM // 2, -sine, sine)
        tabs[2, rows, :] = begin.astype(jnp.float32)

    def forward_weights(phase):
        for way in range(2):
            for copy in w_in(phase, ((1, 2), (3, 4))[way]):
                copy.wait_recv()
            for copy in f_out(phase, way):
                copy.start()

    forward_z(0, range(groups // 2))
    forward_weights(0)
    for copy in w_out(1):
        copy.start()
    forward_z(0, range(groups // 2, groups))
    forward_class(1, range(1, groups))

    def rows_of(h, i, q, first):
        src_d, src_c = i // ctx, i % ctx
        m = (src_d % 2) * 2 + src_c % 2
        s = (src_d // 2) * halves + src_c // 2
        start = pl.multiple_of(h * rows_half + m * slab + s * part + q * piece, piece)
        return acc_ref[pl.ds(start, piece), first : first + HEAD_DIM]

    def rotate(x, at):
        x = x.astype(jnp.bfloat16).astype(jnp.float32)
        turned = pltpu.roll(x, HEAD_DIM // 2, 1)
        cosine = tabs[0, pl.ds(at, 2 * piece), :]
        sine = tabs[1, pl.ds(at, 2 * piece), :]
        return (x * cosine + turned * sine).astype(jnp.bfloat16)

    def pack(half_at, phase):
        @pl.loop(0, devices // 2, unroll=4)
        def _(pair):
            for q in range(quarters):
                def both(first):
                    return jnp.concatenate([rows_of(half_at, pair * 2 + i, q, first) for i in range(2)], axis=0)

                near_at = pl.multiple_of(q * block + pair * 2 * piece, 2 * piece)
                at = pl.multiple_of(half_at * rows_half + near_at, 2 * piece)
                to = pl.ds(at, 2 * piece)
                if phase == 0:
                    key_ref[to, :] = rotate(both(0), at)
                    val_ref[to, :] = both(HEAD_DIM).astype(jnp.bfloat16)
                for h in PHASE_HEADS[phase]:
                    qry_ref[pl.ds(near_at, 2 * piece), h * HEAD_DIM : (h + 1) * HEAD_DIM] = rotate(
                        both((2 + h) * HEAD_DIM), at)

    factor = HEAD_DIM**-0.5 * math.log2(math.e)

    def attend(half_at, phase):
        for j in range(quarters):
            b = half_at * quarters + j
            rows = slice(b * block, (b + 1) * block)
            near_rows = slice(j * block, (j + 1) * block)
            first = max(0, (b * block - (MOST - 1)) // block * block)
            keys = slice(first, (b + 1) * block)
            width = (b + 1) * block - first
            at = first + lax.broadcasted_iota(jnp.int32, (block, width), 1)
            at_own = b * block + lax.broadcasted_iota(jnp.int32, (block, width), 0)
            begin = tabs[2, rows, 0:1]
            allowed = (at.astype(jnp.float32) >= begin) & (at <= at_own)
            for h in PHASE_HEADS[phase]:
                scores = lax.dot_general(
                    qry_ref[near_rows, h * HEAD_DIM : (h + 1) * HEAD_DIM], key_ref[keys, :],
                    (((1,), (1,)), ((), ())), preferred_element_type=jnp.float32,
                )
                scores = jnp.where(allowed, scores, -jnp.inf)
                top = jnp.max(scores, axis=1, keepdims=True)
                weights = jnp.exp2((scores - top) * factor)
                total = jnp.sum(weights, axis=1, keepdims=True)
                mixed = jnp.dot(weights.astype(jnp.bfloat16), val_ref[keys, :],
                                preferred_element_type=jnp.float32)
                mix_ref[near_rows, h * HEAD_DIM : (h + 1) * HEAD_DIM] = mixed / total

    def ret_at(s, m, h, phase):
        return ret_ref.at[pl.ds(pl.multiple_of(s * chunk + h * part, part), part),
                          pl.ds(pl.multiple_of(m * Q_W + phase * RET_W, RET_W), RET_W)]

    def buf_at(i, h, phase):
        return out_buf.at[h, phase, pl.ds(pl.multiple_of(i * part, part), part), :]

    def ret_copy(h, phase, t):
        i = (me + t) % devices
        return remote(buf_at(i, h, phase), ret_at(s_me, m_me, h, phase), r_send.at[h, phase, t],
                      r_recv.at[h, phase, t], (i // ctx, i % ctx))

    def ret_arrival(h, phase, t):
        i = (me - t + devices) % devices
        src_d, src_c = i // ctx, i % ctx
        s = (src_d // 2) * halves + src_c // 2
        m = (src_d % 2) * 2 + src_c % 2
        return remote(buf_at(i, h, phase), ret_at(s, m, h, phase), r_send.at[h, phase, t],
                      r_recv.at[h, phase, t], (src_d, src_c))

    def own_ret(h, phase):
        return pltpu.make_async_copy(buf_at(me, h, phase), ret_at(s_me, m_me, h, phase), r_own.at[h, phase])

    def send_back(h, phase):
        def ready(i):
            parts = [
                mix_ref[pl.ds(pl.multiple_of(q * block + i * piece, piece), piece),
                        phase * RET_W : (phase + 1) * RET_W]
                for q in range(quarters)
            ]
            out_buf[h, phase, pl.ds(pl.multiple_of(i * part, part), part), :] = (
                jnp.concatenate(parts, axis=0).astype(jnp.bfloat16))

        @pl.loop(1, devices)
        def _(t):
            ready((me + t) % devices)
            ret_copy(h, phase, t).start()

        ready(me)
        own_ret(h, phase).start()

    def finish(h, phase):
        pack(h, phase)
        attend(h, phase)
        send_back(h, phase)

    own_copy(0).wait()
    for t in range(groups):
        for which in range(2):
            c_arrival(which, t, 0).wait_recv()
    for copy in w_own:
        copy.wait()

    def multiply(rows, k, start, extent, phase):
        columns = pl.ds(pl.multiple_of(k * depth + start, extent), extent)
        first, width = PHASE_COLUMNS[phase]
        return jnp.dot(x_ref[rows, columns], w_buf[k, start : start + extent, first : first + width],
                       preferred_element_type=jnp.float32)

    def place(phase):
        first, width = PHASE_COLUMNS[phase]
        return slice(first, first + width)

    def whole(rows, phase):
        acc_ref[rows, place(phase)] = multiply(rows, 0, 0, depth, phase)

        @pl.loop(1, dp)
        def _(k):
            acc_ref[rows, place(phase)] += multiply(rows, k, 0, depth, phase)

    early = pl.ds(0, rows_half)
    acc_ref[early, place(0)] = multiply(early, d, 0, depth, 0)
    for copy in w_in(0, (0,)):
        copy.wait_recv()
    for _, d_from in near:
        acc_ref[early, place(0)] += multiply(early, d_from, 0, depth, 0)
    forward_z(1, range(groups // 4))
    for way in range(2):
        for copy in f_in(0, way):
            copy.wait_recv()
        for core in range(2):
            acc_ref[early, place(0)] += multiply(early, chip_far * 2 + core, way * half, half, 0)
    forward_z(1, range(groups // 4, groups // 2))
    forward_weights(1)
    finish(0, 0)

    forward_z(1, range(groups // 2, groups))
    own_copy(1).wait()
    for which in range(2):
        if which:
            for t in range(groups):
                c_arrival(0, t, 1).wait_recv()
                c_arrival(1, t, 1).wait_recv()
        base = (1 - dc if which else dc) * 2 * slab
        whole(pl.ds(pl.multiple_of(rows_half + base, 2 * slab), 2 * slab), 0)
    finish(1, 0)

    for copy in w_in(1, (0,)):
        copy.wait_recv()
    for h in range(2):
        rows = pl.ds(h * rows_half, rows_half)
        acc_ref[rows, place(1)] = multiply(rows, d, 0, depth, 1)
        for _, d_from in near:
            acc_ref[rows, place(1)] += multiply(rows, d_from, 0, depth, 1)
    for copy in f_in(1, 0) + f_in(1, 1):
        copy.wait_recv()
    for h in range(2):
        rows = pl.ds(h * rows_half, rows_half)
        for core in range(2):
            acc_ref[rows, place(1)] += multiply(rows, chip_far * 2 + core, 0, depth, 1)
        finish(h, 1)

    tab_out.wait_send()
    for copy in w_out(0) + w_out(1) + [copy for way in range(2) for phase in range(2) for copy in f_out(phase, way)]:
        copy.wait_send()
    for h in range(2):
        for t in range(groups):
            if t > 0:
                tok_copy(t, h).wait_send()
            z_copy(t, h).wait_send()
            c_copy(0, t, h).wait_send()
            c_copy(1, t, h).wait_send()
        for phase in range(2):
            own_ret(h, phase).wait()

            @pl.loop(1, devices)
            def _(t):
                ret_copy(h, phase, t).wait_send()
                ret_arrival(h, phase, t).wait_recv()


def attended_blocks(slot_of, lengths, tokens, weights, dp, ctx):
    devices, piece, width = tokens.shape
    rows = devices * piece
    depth = weights.shape[0]
    groups = devices // 4
    chunk = rows // groups
    seq = 4 * rows
    dma = pltpu.SemaphoreType.DMA
    return pl.pallas_call(
        functools.partial(whole_kernel, dp, ctx, chunk),
        out_shape=jax.ShapeDtypeStruct((rows, HEADS * HEAD_DIM), jnp.bfloat16),
        in_specs=[
            pl.BlockSpec(memory_space=pltpu.SMEM),
            pl.BlockSpec(memory_space=pltpu.SMEM),
            pl.BlockSpec(memory_space=pltpu.HBM),
            pl.BlockSpec(memory_space=pltpu.HBM),
        ],
        out_specs=pl.BlockSpec(memory_space=pl.ANY),
        scratch_shapes=[
            pltpu.VMEM((devices, piece, width), jnp.bfloat16),
            pltpu.VMEM((rows, width), jnp.bfloat16),
            pltpu.VMEM((2, lengths.shape[1], HEAD_DIM), jnp.int32),
            pltpu.VMEM((seq, width), jnp.bfloat16),
            pltpu.VMEM((dp, depth, PART_W), jnp.bfloat16),
            pltpu.VMEM((seq, PART_W), jnp.float32),
            pltpu.VMEM((seq, HEAD_DIM), jnp.bfloat16),
            pltpu.VMEM((seq, HEAD_DIM), jnp.bfloat16),
            pltpu.VMEM((seq // 2, Q_W), jnp.bfloat16),
            pltpu.VMEM((seq // 2, Q_W), jnp.float32),
            pltpu.VMEM((2, 2, rows * 2, RET_W), jnp.bfloat16),
            pltpu.VMEM((3, seq, HEAD_DIM), jnp.float32),
            dma, dma((2,)), dma((4,)), dma, dma,
            dma((2, groups)), dma((2, groups)),
            dma((2, groups)), dma((2, groups)),
            dma((2, 2, groups)), dma((2, 2, groups)),
            dma((5, 4)), dma((5, 4)),
            dma((2, 2, 4)), dma((2, 2, 4)),
            dma((2, 2)), dma((2, 2, devices)), dma((2, 2, devices)),
        ],
        compiler_params=pltpu.CompilerParams(
            collective_id=0, has_side_effects=True, vmem_limit_bytes=62 * 2**20
        ),
    )(slot_of, lengths, tokens, weights)


def on_device(dp, ctx, tokens, projection, placement, doc_lengths):
    row_count, width = tokens.shape
    dev_count = placement.shape[1]
    piece_rows = row_count // dev_count
    destinations = placement[0]
    index = jnp.arange(dev_count, dtype=jnp.int32)
    slot_of = jnp.sum(jnp.where(destinations[None, :] == index[:, None], index[None, :], 0), axis=1)
    pieces = tokens.reshape(dev_count, piece_rows, width)
    if dp == 8 and ctx == 4 and piece_rows == 8:
        blocks = attended_blocks(slot_of, doc_lengths, pieces, projection, dp, ctx)
    else:
        c = lax.axis_index("ctx")
        arrived = lax.all_to_all(pieces[slot_of], ("dp", "ctx"), split_axis=0, concat_axis=0, tiled=True)
        rows = lax.all_gather(arrived.reshape(row_count, width), "ctx", axis=0, tiled=True)
        cuts = [
            lax.dynamic_slice_in_dim(projection, base + c * w, w, axis=1)
            for base, w in ((0, Q_W), (HEADS * HEAD_DIM, HEAD_DIM), ((HEADS + KV_HEADS) * HEAD_DIM, HEAD_DIM))
        ]
        weights = lax.all_gather(jnp.concatenate(cuts, axis=1), "dp", axis=0, tiled=True)
        projected = jnp.dot(rows, weights, preferred_element_type=jnp.float32).astype(jnp.bfloat16)
        mixed = attention(projected, doc_lengths[0])
        by_source = jnp.transpose(mixed.reshape(ctx, dev_count, piece_rows, Q_W), (1, 0, 2, 3))
        returned = lax.all_to_all(by_source, ("dp", "ctx"), split_axis=0, concat_axis=0, tiled=True)
        parts = returned.reshape(dp, ctx, ctx, piece_rows, Q_W)
        blocks = jnp.transpose(parts, (0, 2, 3, 1, 4))
    blocks = blocks.reshape(dev_count, piece_rows, HEADS * HEAD_DIM)
    return blocks[destinations].reshape(row_count, HEADS * HEAD_DIM)


def solution(mesh):
    return jax.shard_map(
        functools.partial(on_device, mesh.shape["dp"], mesh.shape["ctx"]),
        mesh=mesh,
        in_specs=(P(("dp", "ctx"), None), P("dp", None), P(("dp", "ctx"), None), P("dp", None)),
        out_specs=P(("dp", "ctx"), None),
        check_vma=False,
    )
```

```python
import functools
import math

import jax
import jax.numpy as jnp
from jax import lax
from jax.experimental import pallas as pl
from jax.experimental.pallas import tpu as pltpu
from jax.sharding import PartitionSpec as P

HEAD_DIM = 128
HEADS = 16
KV_HEADS = 4
GROUP = HEADS // KV_HEADS
Q_W = GROUP * HEAD_DIM
PART_W = Q_W + 2 * HEAD_DIM
MOST = 512
MESH = pl.DeviceIdType.MESH

theta_base = 500000.0


def position_tables(lengths, seq):
    position = jnp.arange(seq, dtype=jnp.int32)
    ends = jnp.cumsum(lengths)
    begins = jnp.max(
        jnp.where(position[:, None] >= ends[None, :], ends[None, :], 0), axis=1
    )
    half = HEAD_DIM // 2
    frequency = theta_base ** (-2.0 * jnp.arange(half, dtype=jnp.float32) / HEAD_DIM)
    angles = (position - begins).astype(jnp.float32)[:, None] * frequency[None, :]
    cosine, sine = jnp.cos(angles), jnp.sin(angles)
    return (
        jnp.concatenate([cosine, cosine], axis=1),
        jnp.concatenate([-sine, sine], axis=1),
        jnp.broadcast_to(begins[:, None].astype(jnp.float32), (seq, HEAD_DIM)),
    )


def attention_kernel(block, proj_ref, cos_ref, sin_ref, begin_ref, out_ref, key_ref):
    seq = proj_ref.shape[0]
    factor = HEAD_DIM**-0.5 * math.log2(math.e)

    def rotated(rows, column):
        x = proj_ref[rows, column : column + HEAD_DIM].astype(jnp.float32)
        turned = pltpu.roll(x, HEAD_DIM // 2, 1)
        return (x * cos_ref[rows, :] + turned * sin_ref[rows, :]).astype(jnp.bfloat16)

    for b in range(seq // block):
        rows = slice(b * block, (b + 1) * block)
        key_ref[rows, :] = rotated(rows, Q_W)
    for b in range(seq // block):
        rows = slice(b * block, (b + 1) * block)
        first = max(0, (b * block - (MOST - 1)) // block * block)
        keys = slice(first, (b + 1) * block)
        width = (b + 1) * block - first
        at = first + lax.broadcasted_iota(jnp.int32, (block, width), 1)
        own = b * block + lax.broadcasted_iota(jnp.int32, (block, width), 0)
        allowed = (at.astype(jnp.float32) >= begin_ref[rows, 0:1]) & (at <= own)
        values = proj_ref[keys, Q_W + HEAD_DIM : PART_W]
        for h in range(GROUP):
            scores = lax.dot_general(
                rotated(rows, h * HEAD_DIM),
                key_ref[keys, :],
                (((1,), (1,)), ((), ())),
                preferred_element_type=jnp.float32,
            )
            scores = jnp.where(allowed, scores, -jnp.inf)
            top = jnp.max(scores, axis=1, keepdims=True)
            weights = jnp.exp2((scores - top) * factor)
            total = jnp.sum(weights, axis=1, keepdims=True)
            mixed = jnp.dot(
                weights.astype(jnp.bfloat16), values, preferred_element_type=jnp.float32
            )
            out_ref[rows, h * HEAD_DIM : (h + 1) * HEAD_DIM] = (mixed / total).astype(jnp.bfloat16)


def attention(projected, lengths):
    seq = projected.shape[0]
    cosine, sine, begins = position_tables(lengths, seq)
    return pl.pallas_call(
        functools.partial(attention_kernel, 256),
        out_shape=jax.ShapeDtypeStruct((seq, Q_W), jnp.bfloat16),
        in_specs=[pl.BlockSpec(memory_space=pltpu.VMEM)] * 4,
        out_specs=pl.BlockSpec(memory_space=pltpu.VMEM),
        scratch_shapes=[pltpu.VMEM((seq, HEAD_DIM), jnp.bfloat16)],
        compiler_params=pltpu.CompilerParams(vmem_limit_bytes=32 * 2**20),
    )(projected, cosine, sine, begins)


PHASES = (
    ((HEADS * HEAD_DIM, HEAD_DIM, 0, HEAD_DIM), ((HEADS + KV_HEADS) * HEAD_DIM, HEAD_DIM, HEAD_DIM, HEAD_DIM),
     (0, Q_W, 2 * HEAD_DIM, Q_W // 2)),
    ((Q_W // 2, Q_W, 2 * HEAD_DIM + Q_W // 2, Q_W // 2),),
)

PHASE_COLUMNS = ((0, 2 * HEAD_DIM + Q_W // 2), (2 * HEAD_DIM + Q_W // 2, Q_W // 2))
PHASE_HEADS = (range(0, GROUP // 2), range(GROUP // 2, GROUP))
RET_W = Q_W // 2


def whole_kernel(dp, ctx, chunk, slot_ref, len_ref, tok_hbm, w_ref, ret_ref,
                 tok_ref, stage, ends, x_ref, w_buf, acc_ref, key_ref, val_ref, qry_ref, mix_ref, out_buf, tabs,
                 in_sem, own_sem, wown_sem, tab_send, tab_recv, tok_send, tok_recv, z_send, z_recv,
                 c_send, c_recv, w_send, w_recv, f_send, f_recv, r_own, r_send, r_recv):
    d, c = lax.axis_index("dp"), lax.axis_index("ctx")
    devices = dp * ctx
    me = d * ctx + c
    dc, cz = d % 2, c % 2
    groups = devices // 4
    halves = ctx // 2
    s_me = (d // 2) * halves + c // 2
    m_me = dc * 2 + cz
    m_z = dc * 2 + 1 - cz
    d_sib, c_sib = d + 1 - 2 * dc, c + 1 - 2 * cz
    part = chunk // 2
    slab = groups * part
    depth = w_ref.shape[0]
    piece = chunk // ctx
    block = devices * piece
    seq = ctx * block
    rows_half = seq // 2
    quarters = ctx // 2

    def class_peer(s):
        return ((s // halves) * 2 + dc, (s % halves) * 2 + cz)

    def remote(src, dst, send, recv, device):
        return pltpu.make_async_remote_copy(
            src_ref=src, dst_ref=dst, send_sem=send, recv_sem=recv, device_id=device, device_id_type=MESH
        )

    tok_in = pltpu.make_async_copy(tok_hbm, tok_ref, in_sem)
    tok_in.start()

    barrier = pltpu.get_barrier_semaphore()

    @pl.loop(1, devices)
    def _(t):
        other = (me + t) % devices
        pl.semaphore_signal(barrier, inc=1, device_id=(other // ctx, other % ctx), device_id_type=MESH)

    document = lax.broadcasted_iota(jnp.int32, ends.shape[1:], 0)
    end, table = jnp.int32(0), jnp.zeros(ends.shape[1:], jnp.int32)
    for j in range(ends.shape[1]):
        end = end + len_ref[0, j]
        table = jnp.where(document == j, end, table)
    ends[dc] = table

    pl.semaphore_wait(barrier, devices - 1)

    def gather(s, h):
        at = s * ctx + h * quarters
        rows = [tok_ref[slot_ref[at + q]] for q in range(quarters)]
        start = pl.multiple_of(s * chunk + h * part, part)
        stage[pl.ds(start, part), :] = jnp.concatenate(rows, axis=0)

    def x_rows(m, s, h):
        return x_ref.at[pl.ds(pl.multiple_of(h * rows_half + m * slab + s * part, part), part), :]

    def tok_rows(s, h):
        return stage.at[pl.ds(pl.multiple_of(s * chunk + h * part, part), part), :]

    def own_copy(h):
        return pltpu.make_async_copy(tok_rows(s_me, h), x_rows(m_me, s_me, h), own_sem.at[h])

    def tok_copy(t, h):
        s = (s_me + t) % groups
        return remote(tok_rows(s, h), x_rows(m_me, s_me, h), tok_send.at[h, t], tok_recv.at[h, t], class_peer(s))

    tab_out = remote(ends.at[dc], ends.at[dc], tab_send, tab_recv, (d_sib, c))
    tab_in = remote(ends.at[1 - dc], ends.at[1 - dc], tab_send, tab_recv, (d_sib, c))

    chip = d // 2
    chip_x = chip + 1 - 2 * (chip % 2)
    chip_y = (chip + 2) % 4
    chip_far = (chip_x + 2) % 4

    def w_parts(d_to, d_from, phase):
        g = (d_to % 2) * 2 + cz
        for i, (base, stride, to, width) in enumerate(PHASES[phase]):
            start = pl.multiple_of(base + g * stride, HEAD_DIM)
            yield (w_ref.at[:, pl.ds(start, width)], w_buf.at[d_from, :, to : to + width], 3 * phase + i)

    near = ((0, d_sib), (1, chip_x * 2 + dc), (2, chip_x * 2 + 1 - dc), (3, chip_y * 2 + dc), (4, chip_y * 2 + 1 - dc))

    def w_out(phase, slots=range(5)):
        return [remote(src, dst, w_send.at[slot, i], w_recv.at[slot, i], (d_to, c))
                for slot, d_to in near if slot in slots for src, dst, i in w_parts(d_to, d, phase)]

    def w_in(phase, slots):
        return [remote(src, dst, w_send.at[slot, i], w_recv.at[slot, i], (d_from, c))
                for slot, d_from in near if slot in slots for src, dst, i in w_parts(d, d_from, phase)]

    w_own = [pltpu.make_async_copy(src, dst, wown_sem.at[i])
             for phase in range(2) for src, dst, i in w_parts(d, d, phase)]

    half = depth // 2

    def f_parts(chip_from, way, phase, chip_to):
        for core in range(2):
            for i, (_, _, to, width) in enumerate(PHASES[phase]):
                there = w_buf.at[chip_from * 2 + core, way * half : (way + 1) * half, to : to + width]
                yield remote(there, there, f_send.at[way, core, 3 * phase + i], f_recv.at[way, core, 3 * phase + i],
                             (chip_to * 2 + dc, c))

    def f_out(phase, way):
        return list(f_parts((chip_x, chip_y)[way], way, phase, (chip_y, chip_x)[way]))

    def f_in(phase, way):
        return list(f_parts(chip_far, way, phase, (chip_y, chip_x)[way]))

    def came(t):
        return (s_me - t + groups) % groups

    def tok_arrival(t, h):
        return remote(tok_rows(came(t), h), x_rows(m_me, came(t), h), tok_send.at[h, t], tok_recv.at[h, t],
                      class_peer(came(t)))

    def z_copy(t, h):
        to = x_rows(m_me, came(t), h)
        at = to if t else tok_rows(s_me, h)
        return remote(at, to, z_send.at[h, t], z_recv.at[h, t], (d, c_sib))

    def z_arrival(t, h):
        at = x_rows(m_z, came(t), h)
        return remote(at, at, z_send.at[h, t], z_recv.at[h, t], (d, c_sib))

    def c_copy(which, t, h):
        to = x_rows(m_z if which else m_me, came(t), h)
        at = to if t or which else tok_rows(s_me, h)
        return remote(at, to, c_send.at[h, which, t], c_recv.at[h, which, t], (d_sib, c))

    def c_arrival(which, t, h):
        at = x_rows((1 - dc) * 2 + (1 - cz if which else cz), came(t), h)
        return remote(at, at, c_send.at[h, which, t], c_recv.at[h, which, t], (d_sib, c))

    def forward_class(h, ts):
        for t in ts:
            tok_arrival(t, h).wait_recv()
            z_copy(t, h).start()
            c_copy(0, t, h).start()

    def forward_z(h, ts):
        for t in ts:
            z_arrival(t, h).wait_recv()
            c_copy(1, t, h).start()

    def start_own(h):
        gather(s_me, h)
        z_copy(0, h).start()
        c_copy(0, 0, h).start()
        own_copy(h).start()

    for copy in w_out(0, (1, 3, 2, 4)):
        copy.start()
    tab_out.start()
    tok_in.wait()
    for t in range(1, groups):
        gather((s_me + t) % groups, 0)
        tok_copy(t, 0).start()
        if t == 1:
            start_own(0)
    for copy in w_out(0, (0,)):
        copy.start()
    for copy in w_own:
        copy.start()
    for t in range(1, groups):
        gather((s_me + t) % groups, 1)
    start_own(1)
    forward_class(0, range(1, groups // 2))

    forward_class(0, range(groups // 2, groups))
    for t in range(1, groups):
        tok_copy(t, 1).start()
    for copy in w_out(1):
        copy.start()

    tab_in.wait_recv()

    @pl.loop(0, seq // 64)
    def _(n):
        rows = pl.ds(pl.multiple_of(n * 64, 64), 64)
        position = n * 64 + lax.broadcasted_iota(jnp.int32, (64, HEAD_DIM), 0)
        lane = lax.broadcasted_iota(jnp.int32, (1, HEAD_DIM), 1)
        begin = jnp.zeros((64, HEAD_DIM), jnp.int32)
        for j in range(ends.shape[1]):
            end = ends[c // 2, j : j + 1, :]
            begin = jnp.maximum(begin, jnp.where(position >= end, end, 0))
        spread = (lane % (HEAD_DIM // 2)).astype(jnp.float32) * (-2.0 * math.log(theta_base) / HEAD_DIM)
        angles = (position - begin).astype(jnp.float32) * jnp.exp(spread)
        sine = jnp.sin(angles)
        tabs[0, rows, :] = jnp.cos(angles)
        tabs[1, rows, :] = jnp.where(lane < HEAD_DIM // 2, -sine, sine)
        tabs[2, rows, :] = begin.astype(jnp.float32)

    def forward_weights(phase):
        for way in range(2):
            for copy in w_in(phase, ((1, 2), (3, 4))[way]):
                copy.wait_recv()
            for copy in f_out(phase, way):
                copy.start()

    forward_z(0, range(2))
    forward_weights(0)
    forward_z(0, range(2, groups))
    forward_class(1, range(1, groups))

    def rows_of(h, i, q, first):
        src_d, src_c = i // ctx, i % ctx
        m = (src_d % 2) * 2 + src_c % 2
        s = (src_d // 2) * halves + src_c // 2
        start = pl.multiple_of(h * rows_half + m * slab + s * part + q * piece, piece)
        return acc_ref[pl.ds(start, piece), first : first + HEAD_DIM]

    def rotate(x, at):
        x = x.astype(jnp.bfloat16).astype(jnp.float32)
        turned = pltpu.roll(x, HEAD_DIM // 2, 1)
        cosine = tabs[0, pl.ds(at, 2 * piece), :]
        sine = tabs[1, pl.ds(at, 2 * piece), :]
        return (x * cosine + turned * sine).astype(jnp.bfloat16)

    def pack(half_at, phase):
        @pl.loop(0, devices // 2, unroll=4)
        def _(pair):
            for q in range(quarters):
                def both(first):
                    return jnp.concatenate([rows_of(half_at, pair * 2 + i, q, first) for i in range(2)], axis=0)

                near_at = pl.multiple_of(q * block + pair * 2 * piece, 2 * piece)
                at = pl.multiple_of(half_at * rows_half + near_at, 2 * piece)
                to = pl.ds(at, 2 * piece)
                if phase == 0:
                    key_ref[to, :] = rotate(both(0), at)
                    val_ref[to, :] = both(HEAD_DIM).astype(jnp.bfloat16)
                for h in PHASE_HEADS[phase]:
                    qry_ref[pl.ds(near_at, 2 * piece), h * HEAD_DIM : (h + 1) * HEAD_DIM] = rotate(
                        both((2 + h) * HEAD_DIM), at)

    factor = HEAD_DIM**-0.5 * math.log2(math.e)

    def attend(half_at, phase):
        for j in range(quarters):
            b = half_at * quarters + j
            rows = slice(b * block, (b + 1) * block)
            near_rows = slice(j * block, (j + 1) * block)
            first = max(0, (b * block - (MOST - 1)) // block * block)
            keys = slice(first, (b + 1) * block)
            width = (b + 1) * block - first
            at = first + lax.broadcasted_iota(jnp.int32, (block, width), 1)
            at_own = b * block + lax.broadcasted_iota(jnp.int32, (block, width), 0)
            begin = tabs[2, rows, 0:1]
            allowed = (at.astype(jnp.float32) >= begin) & (at <= at_own)
            for h in PHASE_HEADS[phase]:
                scores = lax.dot_general(
                    qry_ref[near_rows, h * HEAD_DIM : (h + 1) * HEAD_DIM], key_ref[keys, :],
                    (((1,), (1,)), ((), ())), preferred_element_type=jnp.float32,
                )
                scores = jnp.where(allowed, scores, -jnp.inf)
                top = jnp.max(scores, axis=1, keepdims=True)
                weights = jnp.exp2((scores - top) * factor)
                total = jnp.sum(weights, axis=1, keepdims=True)
                mixed = jnp.dot(weights.astype(jnp.bfloat16), val_ref[keys, :],
                                preferred_element_type=jnp.float32)
                mix_ref[near_rows, h * HEAD_DIM : (h + 1) * HEAD_DIM] = mixed / total

    def ret_at(s, m, h, phase):
        return ret_ref.at[pl.ds(pl.multiple_of(s * chunk + h * part, part), part),
                          pl.ds(pl.multiple_of(m * Q_W + phase * RET_W, RET_W), RET_W)]

    def buf_at(i, h, phase):
        return out_buf.at[h, phase, pl.ds(pl.multiple_of(i * part, part), part), :]

    def ret_copy(h, phase, t):
        i = (me + t) % devices
        return remote(buf_at(i, h, phase), ret_at(s_me, m_me, h, phase), r_send.at[h, phase, t],
                      r_recv.at[h, phase, t], (i // ctx, i % ctx))

    def ret_arrival(h, phase, t):
        i = (me - t + devices) % devices
        src_d, src_c = i // ctx, i % ctx
        s = (src_d // 2) * halves + src_c // 2
        m = (src_d % 2) * 2 + src_c % 2
        return remote(buf_at(i, h, phase), ret_at(s, m, h, phase), r_send.at[h, phase, t],
                      r_recv.at[h, phase, t], (src_d, src_c))

    def own_ret(h, phase):
        return pltpu.make_async_copy(buf_at(me, h, phase), ret_at(s_me, m_me, h, phase), r_own.at[h, phase])

    def send_back(h, phase):
        def ready(i):
            parts = [
                mix_ref[pl.ds(pl.multiple_of(q * block + i * piece, piece), piece),
                        phase * RET_W : (phase + 1) * RET_W]
                for q in range(quarters)
            ]
            out_buf[h, phase, pl.ds(pl.multiple_of(i * part, part), part), :] = (
                jnp.concatenate(parts, axis=0).astype(jnp.bfloat16))

        @pl.loop(1, devices)
        def _(t):
            ready((me + t) % devices)
            ret_copy(h, phase, t).start()

        ready(me)
        own_ret(h, phase).start()

    def finish(h, phase):
        pack(h, phase)
        attend(h, phase)
        send_back(h, phase)

    own_copy(0).wait()
    for t in range(groups):
        for which in range(2):
            c_arrival(which, t, 0).wait_recv()
    for copy in w_own:
        copy.wait()

    def multiply(rows, k, start, extent, phase):
        columns = pl.ds(pl.multiple_of(k * depth + start, extent), extent)
        first, width = PHASE_COLUMNS[phase]
        return jnp.dot(x_ref[rows, columns], w_buf[k, start : start + extent, first : first + width],
                       preferred_element_type=jnp.float32)

    def place(phase):
        first, width = PHASE_COLUMNS[phase]
        return slice(first, first + width)

    def whole(rows, phase):
        acc_ref[rows, place(phase)] = multiply(rows, 0, 0, depth, phase)

        @pl.loop(1, dp)
        def _(k):
            acc_ref[rows, place(phase)] += multiply(rows, k, 0, depth, phase)

    early = pl.ds(0, rows_half)
    acc_ref[early, place(0)] = multiply(early, d, 0, depth, 0)
    for copy in w_in(0, (0,)):
        copy.wait_recv()
    for _, d_from in near:
        acc_ref[early, place(0)] += multiply(early, d_from, 0, depth, 0)
    forward_z(1, range(groups // 4))
    forward_weights(1)
    for way in range(2):
        for copy in f_in(0, way):
            copy.wait_recv()
        for core in range(2):
            acc_ref[early, place(0)] += multiply(early, chip_far * 2 + core, way * half, half, 0)
    forward_z(1, range(groups // 4, groups // 2))
    finish(0, 0)

    forward_z(1, range(groups // 2, groups))
    own_copy(1).wait()
    for which in range(2):
        if which:
            for t in range(groups):
                c_arrival(0, t, 1).wait_recv()
                c_arrival(1, t, 1).wait_recv()
        base = (1 - dc if which else dc) * 2 * slab
        whole(pl.ds(pl.multiple_of(rows_half + base, 2 * slab), 2 * slab), 0)
    finish(1, 0)

    for copy in w_in(1, (0,)):
        copy.wait_recv()
    for h in range(2):
        rows = pl.ds(h * rows_half, rows_half)
        acc_ref[rows, place(1)] = multiply(rows, d, 0, depth, 1)
        for _, d_from in near:
            acc_ref[rows, place(1)] += multiply(rows, d_from, 0, depth, 1)
    for copy in f_in(1, 0) + f_in(1, 1):
        copy.wait_recv()
    for h in range(2):
        rows = pl.ds(h * rows_half, rows_half)
        for core in range(2):
            acc_ref[rows, place(1)] += multiply(rows, chip_far * 2 + core, 0, depth, 1)
        finish(h, 1)

    tab_out.wait_send()
    for copy in w_out(0) + w_out(1) + [copy for way in range(2) for phase in range(2) for copy in f_out(phase, way)]:
        copy.wait_send()
    for h in range(2):
        for t in range(groups):
            if t > 0:
                tok_copy(t, h).wait_send()
            z_copy(t, h).wait_send()
            c_copy(0, t, h).wait_send()
            c_copy(1, t, h).wait_send()
        for phase in range(2):
            own_ret(h, phase).wait()

            @pl.loop(1, devices)
            def _(t):
                ret_copy(h, phase, t).wait_send()
                ret_arrival(h, phase, t).wait_recv()


def attended_blocks(slot_of, lengths, tokens, weights, dp, ctx):
    devices, piece, width = tokens.shape
    rows = devices * piece
    depth = weights.shape[0]
    groups = devices // 4
    chunk = rows // groups
    seq = 4 * rows
    dma = pltpu.SemaphoreType.DMA
    return pl.pallas_call(
        functools.partial(whole_kernel, dp, ctx, chunk),
        out_shape=jax.ShapeDtypeStruct((rows, HEADS * HEAD_DIM), jnp.bfloat16),
        in_specs=[
            pl.BlockSpec(memory_space=pltpu.SMEM),
            pl.BlockSpec(memory_space=pltpu.SMEM),
            pl.BlockSpec(memory_space=pltpu.HBM),
            pl.BlockSpec(memory_space=pltpu.HBM),
        ],
        out_specs=pl.BlockSpec(memory_space=pl.ANY),
        scratch_shapes=[
            pltpu.VMEM((devices, piece, width), jnp.bfloat16),
            pltpu.VMEM((rows, width), jnp.bfloat16),
            pltpu.VMEM((2, lengths.shape[1], HEAD_DIM), jnp.int32),
            pltpu.VMEM((seq, width), jnp.bfloat16),
            pltpu.VMEM((dp, depth, PART_W), jnp.bfloat16),
            pltpu.VMEM((seq, PART_W), jnp.float32),
            pltpu.VMEM((seq, HEAD_DIM), jnp.bfloat16),
            pltpu.VMEM((seq, HEAD_DIM), jnp.bfloat16),
            pltpu.VMEM((seq // 2, Q_W), jnp.bfloat16),
            pltpu.VMEM((seq // 2, Q_W), jnp.float32),
            pltpu.VMEM((2, 2, rows * 2, RET_W), jnp.bfloat16),
            pltpu.VMEM((3, seq, HEAD_DIM), jnp.float32),
            dma, dma((2,)), dma((4,)), dma, dma,
            dma((2, groups)), dma((2, groups)),
            dma((2, groups)), dma((2, groups)),
            dma((2, 2, groups)), dma((2, 2, groups)),
            dma((5, 4)), dma((5, 4)),
            dma((2, 2, 4)), dma((2, 2, 4)),
            dma((2, 2)), dma((2, 2, devices)), dma((2, 2, devices)),
        ],
        compiler_params=pltpu.CompilerParams(
            collective_id=0, has_side_effects=True, vmem_limit_bytes=62 * 2**20
        ),
    )(slot_of, lengths, tokens, weights)


def on_device(dp, ctx, tokens, projection, placement, doc_lengths):
    row_count, width = tokens.shape
    dev_count = placement.shape[1]
    piece_rows = row_count // dev_count
    destinations = placement[0]
    index = jnp.arange(dev_count, dtype=jnp.int32)
    slot_of = jnp.sum(jnp.where(destinations[None, :] == index[:, None], index[None, :], 0), axis=1)
    pieces = tokens.reshape(dev_count, piece_rows, width)
    if dp == 8 and ctx == 4 and piece_rows == 8:
        blocks = attended_blocks(slot_of, doc_lengths, pieces, projection, dp, ctx)
    else:
        c = lax.axis_index("ctx")
        arrived = lax.all_to_all(pieces[slot_of], ("dp", "ctx"), split_axis=0, concat_axis=0, tiled=True)
        rows = lax.all_gather(arrived.reshape(row_count, width), "ctx", axis=0, tiled=True)
        cuts = [
            lax.dynamic_slice_in_dim(projection, base + c * w, w, axis=1)
            for base, w in ((0, Q_W), (HEADS * HEAD_DIM, HEAD_DIM), ((HEADS + KV_HEADS) * HEAD_DIM, HEAD_DIM))
        ]
        weights = lax.all_gather(jnp.concatenate(cuts, axis=1), "dp", axis=0, tiled=True)
        projected = jnp.dot(rows, weights, preferred_element_type=jnp.float32).astype(jnp.bfloat16)
        mixed = attention(projected, doc_lengths[0])
        by_source = jnp.transpose(mixed.reshape(ctx, dev_count, piece_rows, Q_W), (1, 0, 2, 3))
        returned = lax.all_to_all(by_source, ("dp", "ctx"), split_axis=0, concat_axis=0, tiled=True)
        parts = returned.reshape(dp, ctx, ctx, piece_rows, Q_W)
        blocks = jnp.transpose(parts, (0, 2, 3, 1, 4))
    blocks = blocks.reshape(dev_count, piece_rows, HEADS * HEAD_DIM)
    return blocks[destinations].reshape(row_count, HEADS * HEAD_DIM)


def solution(mesh):
    return jax.shard_map(
        functools.partial(on_device, mesh.shape["dp"], mesh.shape["ctx"]),
        mesh=mesh,
        in_specs=(P(("dp", "ctx"), None), P("dp", None), P(("dp", "ctx"), None), P("dp", None)),
        out_specs=P(("dp", "ctx"), None),
        check_vma=False,
    )
```

```python
import functools
import math

import jax
import jax.numpy as jnp
from jax import lax
from jax.experimental import pallas as pl
from jax.experimental.pallas import tpu as pltpu
from jax.sharding import PartitionSpec as P

HEAD_DIM = 128
HEADS = 16
KV_HEADS = 4
GROUP = HEADS // KV_HEADS
Q_W = GROUP * HEAD_DIM
PART_W = Q_W + 2 * HEAD_DIM
MOST = 512
MESH = pl.DeviceIdType.MESH

theta_base = 500000.0


def position_tables(lengths, seq):
    position = jnp.arange(seq, dtype=jnp.int32)
    ends = jnp.cumsum(lengths)
    begins = jnp.max(
        jnp.where(position[:, None] >= ends[None, :], ends[None, :], 0), axis=1
    )
    half = HEAD_DIM // 2
    frequency = theta_base ** (-2.0 * jnp.arange(half, dtype=jnp.float32) / HEAD_DIM)
    angles = (position - begins).astype(jnp.float32)[:, None] * frequency[None, :]
    cosine, sine = jnp.cos(angles), jnp.sin(angles)
    return (
        jnp.concatenate([cosine, cosine], axis=1),
        jnp.concatenate([-sine, sine], axis=1),
        jnp.broadcast_to(begins[:, None].astype(jnp.float32), (seq, HEAD_DIM)),
    )


def attention_kernel(block, proj_ref, cos_ref, sin_ref, begin_ref, out_ref, key_ref):
    seq = proj_ref.shape[0]
    factor = HEAD_DIM**-0.5 * math.log2(math.e)

    def rotated(rows, column):
        x = proj_ref[rows, column : column + HEAD_DIM].astype(jnp.float32)
        turned = pltpu.roll(x, HEAD_DIM // 2, 1)
        return (x * cos_ref[rows, :] + turned * sin_ref[rows, :]).astype(jnp.bfloat16)

    for b in range(seq // block):
        rows = slice(b * block, (b + 1) * block)
        key_ref[rows, :] = rotated(rows, Q_W)
    for b in range(seq // block):
        rows = slice(b * block, (b + 1) * block)
        first = max(0, (b * block - (MOST - 1)) // block * block)
        keys = slice(first, (b + 1) * block)
        width = (b + 1) * block - first
        at = first + lax.broadcasted_iota(jnp.int32, (block, width), 1)
        own = b * block + lax.broadcasted_iota(jnp.int32, (block, width), 0)
        allowed = (at.astype(jnp.float32) >= begin_ref[rows, 0:1]) & (at <= own)
        values = proj_ref[keys, Q_W + HEAD_DIM : PART_W]
        for h in range(GROUP):
            scores = lax.dot_general(
                rotated(rows, h * HEAD_DIM),
                key_ref[keys, :],
                (((1,), (1,)), ((), ())),
                preferred_element_type=jnp.float32,
            )
            scores = jnp.where(allowed, scores, -jnp.inf)
            top = jnp.max(scores, axis=1, keepdims=True)
            weights = jnp.exp2((scores - top) * factor)
            total = jnp.sum(weights, axis=1, keepdims=True)
            mixed = jnp.dot(
                weights.astype(jnp.bfloat16), values, preferred_element_type=jnp.float32
            )
            out_ref[rows, h * HEAD_DIM : (h + 1) * HEAD_DIM] = (mixed / total).astype(jnp.bfloat16)


def attention(projected, lengths):
    seq = projected.shape[0]
    cosine, sine, begins = position_tables(lengths, seq)
    return pl.pallas_call(
        functools.partial(attention_kernel, 256),
        out_shape=jax.ShapeDtypeStruct((seq, Q_W), jnp.bfloat16),
        in_specs=[pl.BlockSpec(memory_space=pltpu.VMEM)] * 4,
        out_specs=pl.BlockSpec(memory_space=pltpu.VMEM),
        scratch_shapes=[pltpu.VMEM((seq, HEAD_DIM), jnp.bfloat16)],
        compiler_params=pltpu.CompilerParams(vmem_limit_bytes=32 * 2**20),
    )(projected, cosine, sine, begins)


PHASES = (
    ((HEADS * HEAD_DIM, HEAD_DIM, 0, HEAD_DIM), ((HEADS + KV_HEADS) * HEAD_DIM, HEAD_DIM, HEAD_DIM, HEAD_DIM),
     (0, Q_W, 2 * HEAD_DIM, Q_W // 2)),
    ((Q_W // 2, Q_W, 2 * HEAD_DIM + Q_W // 2, Q_W // 2),),
)

PHASE_COLUMNS = ((0, 2 * HEAD_DIM + Q_W // 2), (2 * HEAD_DIM + Q_W // 2, Q_W // 2))
PHASE_HEADS = (range(0, GROUP // 2), range(GROUP // 2, GROUP))
RET_W = Q_W // 2


def whole_kernel(dp, ctx, chunk, slot_ref, len_ref, tok_hbm, w_ref, ret_ref,
                 tok_ref, stage, ends, x_ref, w_buf, acc_ref, key_ref, val_ref, qry_ref, mix_ref, out_buf, tabs,
                 in_sem, own_sem, wown_sem, tab_send, tab_recv, tok_send, tok_recv, z_send, z_recv,
                 c_send, c_recv, w_send, w_recv, f_send, f_recv, r_own, r_send, r_recv):
    d, c = lax.axis_index("dp"), lax.axis_index("ctx")
    devices = dp * ctx
    me = d * ctx + c
    dc, cz = d % 2, c % 2
    groups = devices // 4
    halves = ctx // 2
    s_me = (d // 2) * halves + c // 2
    m_me = dc * 2 + cz
    m_z = dc * 2 + 1 - cz
    d_sib, c_sib = d + 1 - 2 * dc, c + 1 - 2 * cz
    part = chunk // 2
    slab = groups * part
    depth = w_ref.shape[0]
    piece = chunk // ctx
    block = devices * piece
    seq = ctx * block
    rows_half = seq // 2
    quarters = ctx // 2

    def class_peer(s):
        return ((s // halves) * 2 + dc, (s % halves) * 2 + cz)

    def remote(src, dst, send, recv, device):
        return pltpu.make_async_remote_copy(
            src_ref=src, dst_ref=dst, send_sem=send, recv_sem=recv, device_id=device, device_id_type=MESH
        )

    tok_in = pltpu.make_async_copy(tok_hbm, tok_ref, in_sem)
    tok_in.start()

    barrier = pltpu.get_barrier_semaphore()

    @pl.loop(1, devices)
    def _(t):
        other = (me + t) % devices
        pl.semaphore_signal(barrier, inc=1, device_id=(other // ctx, other % ctx), device_id_type=MESH)

    document = lax.broadcasted_iota(jnp.int32, ends.shape[1:], 0)
    end, table = jnp.int32(0), jnp.zeros(ends.shape[1:], jnp.int32)
    for j in range(ends.shape[1]):
        end = end + len_ref[0, j]
        table = jnp.where(document == j, end, table)
    ends[dc] = table

    pl.semaphore_wait(barrier, devices - 1)

    def gather(s, h):
        at = s * ctx + h * quarters
        rows = [tok_ref[slot_ref[at + q]] for q in range(quarters)]
        start = pl.multiple_of(s * chunk + h * part, part)
        stage[pl.ds(start, part), :] = jnp.concatenate(rows, axis=0)

    def x_rows(m, s, h):
        return x_ref.at[pl.ds(pl.multiple_of(h * rows_half + m * slab + s * part, part), part), :]

    def tok_rows(s, h):
        return stage.at[pl.ds(pl.multiple_of(s * chunk + h * part, part), part), :]

    def own_copy(h):
        return pltpu.make_async_copy(tok_rows(s_me, h), x_rows(m_me, s_me, h), own_sem.at[h])

    def tok_copy(t, h):
        s = (s_me + t) % groups
        return remote(tok_rows(s, h), x_rows(m_me, s_me, h), tok_send.at[h, t], tok_recv.at[h, t], class_peer(s))

    tab_out = remote(ends.at[dc], ends.at[dc], tab_send, tab_recv, (d_sib, c))
    tab_in = remote(ends.at[1 - dc], ends.at[1 - dc], tab_send, tab_recv, (d_sib, c))

    chip = d // 2
    chip_x = chip + 1 - 2 * (chip % 2)
    chip_y = (chip + 2) % 4
    chip_far = (chip_x + 2) % 4

    def w_parts(d_to, d_from, phase):
        g = (d_to % 2) * 2 + cz
        for i, (base, stride, to, width) in enumerate(PHASES[phase]):
            start = pl.multiple_of(base + g * stride, HEAD_DIM)
            yield (w_ref.at[:, pl.ds(start, width)], w_buf.at[d_from, :, to : to + width], 3 * phase + i)

    near = ((0, d_sib), (1, chip_x * 2 + dc), (2, chip_x * 2 + 1 - dc), (3, chip_y * 2 + dc), (4, chip_y * 2 + 1 - dc))

    def w_out(phase, slots=range(5)):
        return [remote(src, dst, w_send.at[slot, i], w_recv.at[slot, i], (d_to, c))
                for slot, d_to in near if slot in slots for src, dst, i in w_parts(d_to, d, phase)]

    def w_in(phase, slots):
        return [remote(src, dst, w_send.at[slot, i], w_recv.at[slot, i], (d_from, c))
                for slot, d_from in near if slot in slots for src, dst, i in w_parts(d, d_from, phase)]

    w_own = [pltpu.make_async_copy(src, dst, wown_sem.at[i])
             for phase in range(2) for src, dst, i in w_parts(d, d, phase)]

    half = depth // 2

    def f_parts(chip_from, way, phase, chip_to):
        for core in range(2):
            for i, (_, _, to, width) in enumerate(PHASES[phase]):
                there = w_buf.at[chip_from * 2 + core, way * half : (way + 1) * half, to : to + width]
                yield remote(there, there, f_send.at[way, core, 3 * phase + i], f_recv.at[way, core, 3 * phase + i],
                             (chip_to * 2 + dc, c))

    def f_out(phase, way):
        return list(f_parts((chip_x, chip_y)[way], way, phase, (chip_y, chip_x)[way]))

    def f_in(phase, way):
        return list(f_parts(chip_far, way, phase, (chip_y, chip_x)[way]))

    def came(t):
        return (s_me - t + groups) % groups

    def tok_arrival(t, h):
        return remote(tok_rows(came(t), h), x_rows(m_me, came(t), h), tok_send.at[h, t], tok_recv.at[h, t],
                      class_peer(came(t)))

    def z_copy(t, h):
        to = x_rows(m_me, came(t), h)
        at = to if t else tok_rows(s_me, h)
        return remote(at, to, z_send.at[h, t], z_recv.at[h, t], (d, c_sib))

    def z_arrival(t, h):
        at = x_rows(m_z, came(t), h)
        return remote(at, at, z_send.at[h, t], z_recv.at[h, t], (d, c_sib))

    def c_copy(which, t, h):
        to = x_rows(m_z if which else m_me, came(t), h)
        at = to if t or which else tok_rows(s_me, h)
        return remote(at, to, c_send.at[h, which, t], c_recv.at[h, which, t], (d_sib, c))

    def c_arrival(which, t, h):
        at = x_rows((1 - dc) * 2 + (1 - cz if which else cz), came(t), h)
        return remote(at, at, c_send.at[h, which, t], c_recv.at[h, which, t], (d_sib, c))

    def forward_class(h, ts):
        for t in ts:
            tok_arrival(t, h).wait_recv()
            z_copy(t, h).start()
            c_copy(0, t, h).start()

    def forward_z(h, ts):
        for t in ts:
            z_arrival(t, h).wait_recv()
            c_copy(1, t, h).start()

    def start_own(h):
        gather(s_me, h)
        z_copy(0, h).start()
        c_copy(0, 0, h).start()
        own_copy(h).start()

    tab_out.start()
    tok_in.wait()
    for t in range(1, groups):
        gather((s_me + t) % groups, 0)
        tok_copy(t, 0).start()
        if t == 1:
            start_own(0)
    for t in range(1, groups):
        gather((s_me + t) % groups, 1)
        tok_copy(t, 1).start()
        if t == 1:
            start_own(1)
    forward_class(0, range(1, groups // 2))
    for copy in w_out(0, (1, 3, 2, 4, 0)):
        copy.start()
    for copy in w_own:
        copy.start()

    forward_class(0, range(groups // 2, groups))

    tab_in.wait_recv()

    @pl.loop(0, seq // 64)
    def _(n):
        rows = pl.ds(pl.multiple_of(n * 64, 64), 64)
        position = n * 64 + lax.broadcasted_iota(jnp.int32, (64, HEAD_DIM), 0)
        lane = lax.broadcasted_iota(jnp.int32, (1, HEAD_DIM), 1)
        begin = jnp.zeros((64, HEAD_DIM), jnp.int32)
        for j in range(ends.shape[1]):
            end = ends[c // 2, j : j + 1, :]
            begin = jnp.maximum(begin, jnp.where(position >= end, end, 0))
        spread = (lane % (HEAD_DIM // 2)).astype(jnp.float32) * (-2.0 * math.log(theta_base) / HEAD_DIM)
        angles = (position - begin).astype(jnp.float32) * jnp.exp(spread)
        sine = jnp.sin(angles)
        tabs[0, rows, :] = jnp.cos(angles)
        tabs[1, rows, :] = jnp.where(lane < HEAD_DIM // 2, -sine, sine)
        tabs[2, rows, :] = begin.astype(jnp.float32)

    def forward_weights(phase):
        for way in range(2):
            for copy in w_in(phase, ((1, 2), (3, 4))[way]):
                copy.wait_recv()
            for copy in f_out(phase, way):
                copy.start()

    forward_z(0, range(groups // 2))
    forward_weights(0)
    for copy in w_out(1):
        copy.start()
    forward_z(0, range(groups // 2, groups))
    forward_class(1, range(1, groups))

    def rows_of(h, i, q, first):
        src_d, src_c = i // ctx, i % ctx
        m = (src_d % 2) * 2 + src_c % 2
        s = (src_d // 2) * halves + src_c // 2
        start = pl.multiple_of(h * rows_half + m * slab + s * part + q * piece, piece)
        return acc_ref[pl.ds(start, piece), first : first + HEAD_DIM]

    def rotate(x, at):
        x = x.astype(jnp.bfloat16).astype(jnp.float32)
        turned = pltpu.roll(x, HEAD_DIM // 2, 1)
        cosine = tabs[0, pl.ds(at, 2 * piece), :]
        sine = tabs[1, pl.ds(at, 2 * piece), :]
        return (x * cosine + turned * sine).astype(jnp.bfloat16)

    def pack(half_at, phase):
        @pl.loop(0, devices // 2, unroll=4)
        def _(pair):
            for q in range(quarters):
                def both(first):
                    return jnp.concatenate([rows_of(half_at, pair * 2 + i, q, first) for i in range(2)], axis=0)

                near_at = pl.multiple_of(q * block + pair * 2 * piece, 2 * piece)
                at = pl.multiple_of(half_at * rows_half + near_at, 2 * piece)
                to = pl.ds(at, 2 * piece)
                if phase == 0:
                    key_ref[to, :] = rotate(both(0), at)
                    val_ref[to, :] = both(HEAD_DIM).astype(jnp.bfloat16)
                for h in PHASE_HEADS[phase]:
                    qry_ref[pl.ds(near_at, 2 * piece), h * HEAD_DIM : (h + 1) * HEAD_DIM] = rotate(
                        both((2 + h) * HEAD_DIM), at)

    factor = HEAD_DIM**-0.5 * math.log2(math.e)

    def attend(half_at, phase):
        for j in range(quarters):
            b = half_at * quarters + j
            rows = slice(b * block, (b + 1) * block)
            near_rows = slice(j * block, (j + 1) * block)
            first = max(0, (b * block - (MOST - 1)) // block * block)
            keys = slice(first, (b + 1) * block)
            width = (b + 1) * block - first
            at = first + lax.broadcasted_iota(jnp.int32, (block, width), 1)
            at_own = b * block + lax.broadcasted_iota(jnp.int32, (block, width), 0)
            begin = tabs[2, rows, 0:1]
            allowed = (at.astype(jnp.float32) >= begin) & (at <= at_own)
            for h in PHASE_HEADS[phase]:
                scores = lax.dot_general(
                    qry_ref[near_rows, h * HEAD_DIM : (h + 1) * HEAD_DIM], key_ref[keys, :],
                    (((1,), (1,)), ((), ())), preferred_element_type=jnp.float32,
                )
                scores = jnp.where(allowed, scores, -jnp.inf)
                top = jnp.max(scores, axis=1, keepdims=True)
                weights = jnp.exp2((scores - top) * factor)
                total = jnp.sum(weights, axis=1, keepdims=True)
                mixed = jnp.dot(weights.astype(jnp.bfloat16), val_ref[keys, :],
                                preferred_element_type=jnp.float32)
                mix_ref[near_rows, h * HEAD_DIM : (h + 1) * HEAD_DIM] = mixed / total

    def ret_at(s, m, h, phase):
        return ret_ref.at[pl.ds(pl.multiple_of(s * chunk + h * part, part), part),
                          pl.ds(pl.multiple_of(m * Q_W + phase * RET_W, RET_W), RET_W)]

    def buf_at(i, h, phase):
        return out_buf.at[h, phase, pl.ds(pl.multiple_of(i * part, part), part), :]

    def ret_copy(h, phase, t):
        i = (me + t) % devices
        return remote(buf_at(i, h, phase), ret_at(s_me, m_me, h, phase), r_send.at[h, phase, t],
                      r_recv.at[h, phase, t], (i // ctx, i % ctx))

    def ret_arrival(h, phase, t):
        i = (me - t + devices) % devices
        src_d, src_c = i // ctx, i % ctx
        s = (src_d // 2) * halves + src_c // 2
        m = (src_d % 2) * 2 + src_c % 2
        return remote(buf_at(i, h, phase), ret_at(s, m, h, phase), r_send.at[h, phase, t],
                      r_recv.at[h, phase, t], (src_d, src_c))

    def own_ret(h, phase):
        return pltpu.make_async_copy(buf_at(me, h, phase), ret_at(s_me, m_me, h, phase), r_own.at[h, phase])

    def send_back(h, phase):
        def ready(i):
            parts = [
                mix_ref[pl.ds(pl.multiple_of(q * block + i * piece, piece), piece),
                        phase * RET_W : (phase + 1) * RET_W]
                for q in range(quarters)
            ]
            out_buf[h, phase, pl.ds(pl.multiple_of(i * part, part), part), :] = (
                jnp.concatenate(parts, axis=0).astype(jnp.bfloat16))

        @pl.loop(1, devices)
        def _(t):
            ready((me + t) % devices)
            ret_copy(h, phase, t).start()

        ready(me)
        own_ret(h, phase).start()

    def finish(h, phase):
        pack(h, phase)
        attend(h, phase)
        send_back(h, phase)

    own_copy(0).wait()
    for t in range(groups):
        for which in range(2):
            c_arrival(which, t, 0).wait_recv()
    for copy in w_own:
        copy.wait()

    def multiply(rows, k, start, extent, phase):
        columns = pl.ds(pl.multiple_of(k * depth + start, extent), extent)
        first, width = PHASE_COLUMNS[phase]
        return jnp.dot(x_ref[rows, columns], w_buf[k, start : start + extent, first : first + width],
                       preferred_element_type=jnp.float32)

    def place(phase):
        first, width = PHASE_COLUMNS[phase]
        return slice(first, first + width)

    def whole(rows, phase):
        acc_ref[rows, place(phase)] = multiply(rows, 0, 0, depth, phase)

        @pl.loop(1, dp)
        def _(k):
            acc_ref[rows, place(phase)] += multiply(rows, k, 0, depth, phase)

    early = pl.ds(0, rows_half)
    acc_ref[early, place(0)] = multiply(early, d, 0, depth, 0)
    for copy in w_in(0, (0,)):
        copy.wait_recv()
    for _, d_from in near:
        acc_ref[early, place(0)] += multiply(early, d_from, 0, depth, 0)
    forward_z(1, range(groups // 4))
    for way in range(2):
        for copy in f_in(0, way):
            copy.wait_recv()
        for core in range(2):
            acc_ref[early, place(0)] += multiply(early, chip_far * 2 + core, way * half, half, 0)
    forward_z(1, range(groups // 4, groups // 2))
    forward_weights(1)
    finish(0, 0)

    forward_z(1, range(groups // 2, groups))
    own_copy(1).wait()
    for which in range(2):
        if which:
            for t in range(groups):
                c_arrival(0, t, 1).wait_recv()
                c_arrival(1, t, 1).wait_recv()
        base = (1 - dc if which else dc) * 2 * slab
        whole(pl.ds(pl.multiple_of(rows_half + base, 2 * slab), 2 * slab), 0)
    finish(1, 0)

    for copy in w_in(1, (0,)):
        copy.wait_recv()
    for h in range(2):
        rows = pl.ds(h * rows_half, rows_half)
        acc_ref[rows, place(1)] = multiply(rows, d, 0, depth, 1)
        for _, d_from in near:
            acc_ref[rows, place(1)] += multiply(rows, d_from, 0, depth, 1)
    for copy in f_in(1, 0) + f_in(1, 1):
        copy.wait_recv()
    for h in range(2):
        rows = pl.ds(h * rows_half, rows_half)
        for core in range(2):
            acc_ref[rows, place(1)] += multiply(rows, chip_far * 2 + core, 0, depth, 1)
        finish(h, 1)

    tab_out.wait_send()
    for copy in w_out(0) + w_out(1) + [copy for way in range(2) for phase in range(2) for copy in f_out(phase, way)]:
        copy.wait_send()
    for h in range(2):
        for t in range(groups):
            if t > 0:
                tok_copy(t, h).wait_send()
            z_copy(t, h).wait_send()
            c_copy(0, t, h).wait_send()
            c_copy(1, t, h).wait_send()
        for phase in range(2):
            own_ret(h, phase).wait()

            @pl.loop(1, devices)
            def _(t):
                ret_copy(h, phase, t).wait_send()
                ret_arrival(h, phase, t).wait_recv()


def attended_blocks(slot_of, lengths, tokens, weights, dp, ctx):
    devices, piece, width = tokens.shape
    rows = devices * piece
    depth = weights.shape[0]
    groups = devices // 4
    chunk = rows // groups
    seq = 4 * rows
    dma = pltpu.SemaphoreType.DMA
    return pl.pallas_call(
        functools.partial(whole_kernel, dp, ctx, chunk),
        out_shape=jax.ShapeDtypeStruct((rows, HEADS * HEAD_DIM), jnp.bfloat16),
        in_specs=[
            pl.BlockSpec(memory_space=pltpu.SMEM),
            pl.BlockSpec(memory_space=pltpu.SMEM),
            pl.BlockSpec(memory_space=pltpu.HBM),
            pl.BlockSpec(memory_space=pltpu.HBM),
        ],
        out_specs=pl.BlockSpec(memory_space=pl.ANY),
        scratch_shapes=[
            pltpu.VMEM((devices, piece, width), jnp.bfloat16),
            pltpu.VMEM((rows, width), jnp.bfloat16),
            pltpu.VMEM((2, lengths.shape[1], HEAD_DIM), jnp.int32),
            pltpu.VMEM((seq, width), jnp.bfloat16),
            pltpu.VMEM((dp, depth, PART_W), jnp.bfloat16),
            pltpu.VMEM((seq, PART_W), jnp.float32),
            pltpu.VMEM((seq, HEAD_DIM), jnp.bfloat16),
            pltpu.VMEM((seq, HEAD_DIM), jnp.bfloat16),
            pltpu.VMEM((seq // 2, Q_W), jnp.bfloat16),
            pltpu.VMEM((seq // 2, Q_W), jnp.float32),
            pltpu.VMEM((2, 2, rows * 2, RET_W), jnp.bfloat16),
            pltpu.VMEM((3, seq, HEAD_DIM), jnp.float32),
            dma, dma((2,)), dma((4,)), dma, dma,
            dma((2, groups)), dma((2, groups)),
            dma((2, groups)), dma((2, groups)),
            dma((2, 2, groups)), dma((2, 2, groups)),
            dma((5, 4)), dma((5, 4)),
            dma((2, 2, 4)), dma((2, 2, 4)),
            dma((2, 2)), dma((2, 2, devices)), dma((2, 2, devices)),
        ],
        compiler_params=pltpu.CompilerParams(
            collective_id=0, has_side_effects=True, vmem_limit_bytes=48 * 2**20
        ),
    )(slot_of, lengths, tokens, weights)


def on_device(dp, ctx, tokens, projection, placement, doc_lengths):
    row_count, width = tokens.shape
    dev_count = placement.shape[1]
    piece_rows = row_count // dev_count
    destinations = placement[0]
    index = jnp.arange(dev_count, dtype=jnp.int32)
    slot_of = jnp.sum(jnp.where(destinations[None, :] == index[:, None], index[None, :], 0), axis=1)
    pieces = tokens.reshape(dev_count, piece_rows, width)
    if dp == 8 and ctx == 4 and piece_rows == 8:
        blocks = attended_blocks(slot_of, doc_lengths, pieces, projection, dp, ctx)
    else:
        c = lax.axis_index("ctx")
        arrived = lax.all_to_all(pieces[slot_of], ("dp", "ctx"), split_axis=0, concat_axis=0, tiled=True)
        rows = lax.all_gather(arrived.reshape(row_count, width), "ctx", axis=0, tiled=True)
        cuts = [
            lax.dynamic_slice_in_dim(projection, base + c * w, w, axis=1)
            for base, w in ((0, Q_W), (HEADS * HEAD_DIM, HEAD_DIM), ((HEADS + KV_HEADS) * HEAD_DIM, HEAD_DIM))
        ]
        weights = lax.all_gather(jnp.concatenate(cuts, axis=1), "dp", axis=0, tiled=True)
        projected = jnp.dot(rows, weights, preferred_element_type=jnp.float32).astype(jnp.bfloat16)
        mixed = attention(projected, doc_lengths[0])
        by_source = jnp.transpose(mixed.reshape(ctx, dev_count, piece_rows, Q_W), (1, 0, 2, 3))
        returned = lax.all_to_all(by_source, ("dp", "ctx"), split_axis=0, concat_axis=0, tiled=True)
        parts = returned.reshape(dp, ctx, ctx, piece_rows, Q_W)
        blocks = jnp.transpose(parts, (0, 2, 3, 1, 4))
    blocks = blocks.reshape(dev_count, piece_rows, HEADS * HEAD_DIM)
    return blocks[destinations].reshape(row_count, HEADS * HEAD_DIM)


def solution(mesh):
    return jax.shard_map(
        functools.partial(on_device, mesh.shape["dp"], mesh.shape["ctx"]),
        mesh=mesh,
        in_specs=(P(("dp", "ctx"), None), P("dp", None), P(("dp", "ctx"), None), P("dp", None)),
        out_specs=P(("dp", "ctx"), None),
        check_vma=False,
    )
```
